256 devices in a mesh: seq: 32 (over z_lo, y, x), head: 8 (over z_hi, core).
Axes of the slice: x: 4, y: 4, z: 8 (z_hi: 4, z_lo: 2; z = z_hi * 2 + z_lo), core: 2. Of those that a mesh axis runs over, the one named last changes fastest.
Arguments:
- prompt_q: bfloat16 [2048, 8192], P(('seq', 'head')), may hold values from -100 to 100
- prompt_k: bfloat16 [2048, 1024], P(('seq', 'head')), may hold values from -4 to 4
- prompt_v: bfloat16 [2048, 1024], P(('seq', 'head')), may hold values from -6 to 6
- prompt_dout: bfloat16 [2048, 8192], P(('seq', 'head')), may hold values from -6 to 6
- cand_q: bfloat16 [8192, 8192], P(('seq', 'head')), may hold values from -100 to 100
- cand_k: bfloat16 [8192, 1024], P(('seq', 'head')), may hold values from -6 to 6
- cand_v: bfloat16 [8192, 1024], P(('seq', 'head')), may hold values from -6 to 6
- cand_dout: bfloat16 [8192, 8192], P(('seq', 'head')), may hold values from -6 to 6
- cand_len: int32 [16], replicated, may hold values from 128 to 512, as said below
- placement: int32 [16], replicated, may hold values from 0 to 15, each once
Outputs:
- prompt_out: bfloat16 [2048, 8192], P(('seq', 'head'))
- prompt_dq: bfloat16 [2048, 8192], P(('seq', 'head'))
- prompt_dk: bfloat16 [2048, 1024], P(('seq', 'head'))
- prompt_dv: bfloat16 [2048, 1024], P(('seq', 'head'))
- cand_out: bfloat16 [8192, 8192], P(('seq', 'head'))
- cand_dq: bfloat16 [8192, 8192], P(('seq', 'head'))
- cand_dk: bfloat16 [8192, 1024], P(('seq', 'head'))
- cand_dv: bfloat16 [8192, 1024], P(('seq', 'head'))
The draws below stay inside these ranges and needn't reach their ends.
Inputs may be any that keep to these rules, and one draw needn't show every extreme that they name: `cand_len`: some candidate has 512 tokens and some has 128.
All inputs are finite; a program needn't handle non-finite values.
Results may differ from the reference program's by a relative error of at most 0.012.
The reference program's roundings to bfloat16 on the way count: a program that leaves them out, or rounds other values in their place, can miss the bound.
Values may be sent and summed in bfloat16 or wider, within the bound.
A program may use at most 64 MiB of HBM per device.

```python
import math
import jax
import jax.numpy as jnp
from jax import lax

HEADS = 64
KV_HEADS = 8
HD = 128
PROMPT = 2048
SPAN = 512
CANDS = 16
CTOK = 8192


def shared_keys(key):
    return jnp.clip(jax.random.normal(jax.random.fold_in(key, 11), (PROMPT, KV_HEADS * HD), jnp.float32), -4.0, 4.0)


def draw_prompt_k(key, part):
    shared = shared_keys(key)
    return shared.astype(jnp.bfloat16)


def draw_prompt_q(key, part):
    key = jax.random.fold_in(key, 5)
    rows = jnp.clip(jax.random.normal(key, (PROMPT, HEADS * HD), jnp.float32), -5.0, 5.0)
    return rows.astype(jnp.bfloat16)


def draw_cand_q(key, part):
    key = jax.random.fold_in(key, 9)
    rows = jnp.clip(jax.random.normal(key, (CTOK, HEADS * HD), jnp.float32), -5.0, 5.0)
    return rows.astype(jnp.bfloat16)


def draw_cand_len(key, part):
    key = jax.random.fold_in(key, 7)
    first_key, second_key, third_key = jax.random.split(key, 3)
    lengths = jax.random.randint(first_key, (CANDS,), SPAN // 4, SPAN + 1)
    longest = jax.random.randint(second_key, (), 0, CANDS)
    shortest = (longest + 1 + jax.random.randint(third_key, (), 0, CANDS - 1)) % CANDS
    lengths = lengths.at[longest].set(SPAN).at[shortest].set(SPAN // 4)
    return lengths.astype(jnp.int32)


def levels(rng, dims, pieces, least, high):
    loudness = 1.0
    for axis_at, shards_of in pieces:
        steps = jax.random.uniform(jax.random.fold_in(jax.random.fold_in(rng, 6), axis_at), (shards_of,), jnp.float32, least / len(pieces), high / len(pieces))
        loudness = loudness * jnp.repeat(jnp.exp(steps), dims[axis_at] // shards_of).reshape((-1,) + (1,) * (len(dims) - 1 - axis_at))
    return loudness


def bell_draw(rng, dims, spread, reach, cuts=(), kind=jnp.bfloat16):
    array = spread * jax.random.normal(rng, dims, jnp.float32)
    if cuts:
        array = array * levels(rng, dims, cuts, -0.22, 0.18)
    return jnp.clip(array, -reach, reach).astype(kind)


def setup_inputs(seed: int = 0) -> dict:
    arg_keys = jax.random.split(jax.random.key(seed), 11)
    return {
        "prompt_q": draw_prompt_q(jax.random.fold_in(arg_keys[10], 71), 0),
        "prompt_k": draw_prompt_k(jax.random.fold_in(arg_keys[10], 71), 0),
        "prompt_v": bell_draw(arg_keys[2], (PROMPT, KV_HEADS * HD), 1.0, 6.0, ((0, 256),)),
        "prompt_dout": bell_draw(arg_keys[3], (PROMPT, HEADS * HD), 1.0, 6.0, ((0, 256),)),
        "cand_q": draw_cand_q(jax.random.fold_in(arg_keys[10], 71), 0),
        "cand_k": bell_draw(arg_keys[5], (CTOK, KV_HEADS * HD), 1.0, 6.0, ((0, 256),)),
        "cand_v": bell_draw(arg_keys[6], (CTOK, KV_HEADS * HD), 1.0, 6.0, ((0, 256),)),
        "cand_dout": bell_draw(arg_keys[7], (CTOK, HEADS * HD), 1.0, 6.0, ((0, 256),)),
        "cand_len": draw_cand_len(jax.random.fold_in(arg_keys[10], 71), 0),
        "placement": jax.random.permutation(arg_keys[9], CANDS).astype(jnp.int32),
    }


def head_pass(queries, key_rows, value_rows, out_grads, allowed, is_valid):
    scaling = 1.0 / math.sqrt(queries.shape[-1])
    scores = jnp.dot(queries, key_rows.T, preferred_element_type=jnp.float32) * scaling
    scores = jnp.where(allowed, scores, -1e+30)
    row_peak = lax.optimization_barrier(jnp.max(scores, axis=1, keepdims=True))
    row_total = lax.optimization_barrier(jnp.sum(jnp.exp(scores - row_peak), axis=1, keepdims=True))
    log_total = row_peak + jnp.log(row_total)
    weights = jnp.exp(scores - log_total)
    weight_half = weights.astype(jnp.bfloat16)
    product = jnp.dot(weight_half, value_rows, preferred_element_type=jnp.float32)
    output = jnp.where(is_valid[:, None], product, 0.0)
    row_delta = lax.optimization_barrier(jnp.sum(out_grads.astype(jnp.float32) * output, axis=1, keepdims=True))
    grad_weights = jnp.dot(out_grads, value_rows.T, preferred_element_type=jnp.float32)
    grad_scores = (weights * (grad_weights - row_delta)).astype(jnp.bfloat16)
    query_grad = (scaling * jnp.dot(grad_scores, key_rows, preferred_element_type=jnp.float32)).astype(jnp.bfloat16)
    key_grad = scaling * jnp.dot(grad_scores.T, queries, preferred_element_type=jnp.float32)
    value_grad = jnp.dot(weight_half.T, out_grads, preferred_element_type=jnp.float32)
    return (output.astype(jnp.bfloat16), query_grad, key_grad, value_grad)

def reference(prompt_q, prompt_k, prompt_v, prompt_dout, cand_q, cand_k, cand_v, cand_dout, cand_len, placement):
    group_size = HEADS // KV_HEADS
    slot_ids = jnp.arange(CANDS, dtype=jnp.int32)
    slot_length = lax.optimization_barrier(jnp.sum(jnp.where(placement[None, :] == slot_ids[:, None], cand_len[None, :], 0), axis=1))
    positions = jnp.arange(SPAN, dtype=jnp.int32)
    is_valid = positions[None, :] < slot_length[:, None]
    prompt_rows = jnp.arange(PROMPT, dtype=jnp.int32)
    prompt_allowed = prompt_rows[None, :] <= prompt_rows[:, None]
    prompt_valid = jnp.ones((PROMPT,), bool)
    cand_allowed = jnp.concatenate([jnp.ones((SPAN, PROMPT), bool), positions[None, :] <= positions[:, None]], axis=1)
    live_grads = jnp.where(is_valid.reshape(CTOK, 1), cand_dout, jnp.zeros_like(cand_dout))
    batched = jax.vmap(head_pass, in_axes=(0, 0, 0, 0, None, 0))

    def per_kv(kv_index):
        key_col = kv_index * HD
        prompt_keys = lax.dynamic_slice_in_dim(prompt_k, key_col, HD, 1)
        prompt_vals = lax.dynamic_slice_in_dim(prompt_v, key_col, HD, 1)
        cand_keys = lax.dynamic_slice_in_dim(cand_k, key_col, HD, 1).reshape(CANDS, SPAN, HD)
        cand_vals = lax.dynamic_slice_in_dim(cand_v, key_col, HD, 1).reshape(CANDS, SPAN, HD)
        slot_keys = jnp.concatenate([jnp.broadcast_to(prompt_keys[None], (CANDS, PROMPT, HD)), cand_keys], axis=1)
        slot_vals = jnp.concatenate([jnp.broadcast_to(prompt_vals[None], (CANDS, PROMPT, HD)), cand_vals], axis=1)

        def per_query(carry, inner):
            column = (kv_index * group_size + inner) * HD
            p_query = lax.dynamic_slice_in_dim(prompt_q, column, HD, 1)
            p_grad = lax.dynamic_slice_in_dim(prompt_dout, column, HD, 1)
            c_query = lax.dynamic_slice_in_dim(cand_q, column, HD, 1).reshape(CANDS, SPAN, HD)
            c_grad = lax.dynamic_slice_in_dim(live_grads, column, HD, 1).reshape(CANDS, SPAN, HD)
            p_out, p_dq, p_dk, p_dv = head_pass(p_query, prompt_keys, prompt_vals, p_grad, prompt_allowed, prompt_valid)
            c_out, c_dq, c_dk, c_dv = batched(c_query, slot_keys, slot_vals, c_grad, cand_allowed, is_valid)
            acc_pk, acc_pv, acc_ck, acc_cv = carry
            acc_pk = acc_pk + p_dk + lax.optimization_barrier(jnp.sum(c_dk[:, :PROMPT], axis=0))
            acc_pv = acc_pv + p_dv + lax.optimization_barrier(jnp.sum(c_dv[:, :PROMPT], axis=0))
            acc_ck = acc_ck + c_dk[:, PROMPT:]
            acc_cv = acc_cv + c_dv[:, PROMPT:]
            return ((acc_pk, acc_pv, acc_ck, acc_cv), (p_out, p_dq, c_out.reshape(CTOK, HD), c_dq.reshape(CTOK, HD)))
        start = (jnp.zeros((PROMPT, HD), jnp.float32), jnp.zeros((PROMPT, HD), jnp.float32), jnp.zeros((CANDS, SPAN, HD), jnp.float32), jnp.zeros((CANDS, SPAN, HD), jnp.float32))
        carry, stacked = lax.scan(per_query, start, jnp.arange(group_size, dtype=jnp.int32))
        return (stacked[0], stacked[1], stacked[2], stacked[3], carry[0].astype(jnp.bfloat16), carry[1].astype(jnp.bfloat16), carry[2].astype(jnp.bfloat16), carry[3].astype(jnp.bfloat16))
    p_out, p_dq, c_out, c_dq, p_dk, p_dv, c_dk, c_dv = lax.map(per_kv, jnp.arange(KV_HEADS, dtype=jnp.int32))
    prompt_out = jnp.transpose(p_out, (2, 0, 1, 3)).reshape(PROMPT, HEADS * HD)
    prompt_dq = jnp.transpose(p_dq, (2, 0, 1, 3)).reshape(PROMPT, HEADS * HD)
    cand_out = jnp.transpose(c_out, (2, 0, 1, 3)).reshape(CTOK, HEADS * HD)
    cand_dq = jnp.transpose(c_dq, (2, 0, 1, 3)).reshape(CTOK, HEADS * HD)
    prompt_dk = jnp.transpose(p_dk, (1, 0, 2)).reshape(PROMPT, KV_HEADS * HD)
    prompt_dv = jnp.transpose(p_dv, (1, 0, 2)).reshape(PROMPT, KV_HEADS * HD)
    cand_dk = jnp.transpose(c_dk, (1, 2, 0, 3)).reshape(CTOK, KV_HEADS * HD)
    cand_dv = jnp.transpose(c_dv, (1, 2, 0, 3)).reshape(CTOK, KV_HEADS * HD)
    return (prompt_out, prompt_dq, prompt_dk, prompt_dv, cand_out, cand_dq, cand_dk, cand_dv)
```

```python
import functools
import math

import jax
import jax.numpy as jnp
from jax import lax
from jax.experimental import pallas as pl
from jax.experimental.pallas import tpu as pltpu
from jax.sharding import PartitionSpec as P

HD = 128
SCALE = 1.0 / math.sqrt(HD)
SCALE2 = SCALE * math.log2(math.e)
MESH = pl.DeviceIdType.MESH
f32, bf16 = jnp.float32, jnp.bfloat16
HIDDEN = -1e30


def coords():
    seq, head = lax.axis_index("seq"), lax.axis_index("head")
    x, y = seq % 4, (seq // 4) % 4
    z = (head // 2) * 2 + seq // 16
    return x, y, z, head % 2


def device(x, y, z, core):
    return ((z % 2) * 16 + y * 4 + x, (z // 2) * 2 + core)


def roles(x, y, core):
    xg, sx, yg, sy = x // 2, x % 2, y // 2, y % 2
    j = sy * 4 + sx * 2 + core
    g = ((sy + yg) % 2) * 4 + ((sx + xg) % 2) * 2 + core
    return xg, yg, j, g


def flip(value, bits):
    out = 0
    for bit in (4, 2, 1):
        digit = (value // bit) % 2
        out = out + bit * ((1 - digit) if bits & bit else digit)
    return out


def block_partner(x, y, z, core, d):
    px = x // 2 * 2 + (1 - x % 2 if d & 2 else x % 2)
    py = y // 2 * 2 + (1 - y % 2 if d & 4 else y % 2)
    return device(px, py, z, 1 - core if d & 1 else core)


def greet(partners):
    barrier = pltpu.get_barrier_semaphore()
    for partner in partners:
        pl.semaphore_signal(barrier, inc=1, device_id=partner, device_id_type=MESH)
    pl.semaphore_wait(barrier, len(partners))


def remote(src, dst, send, recv, target):
    return pltpu.make_async_remote_copy(
        src_ref=src, dst_ref=dst, send_sem=send, recv_sem=recv, device_id=target, device_id_type=MESH
    )


def gather_kernel(qd, kvp, kvc, qd_out, kvp_out, kvc_out, own, sends, recvs, psend, precv, csend, crecv):
    x, y, z, core = coords()
    xg, yg, j, g = roles(x, y, core)
    zhi = z // 2
    block = {d: block_partner(x, y, z, core, d) for d in range(1, 8)}
    mirror = (device(3 - x, y, z, core), device(x, 3 - y, z, core), device(3 - x, 3 - y, z, core))
    up, down = device(x, y, (z + 1) % 8, core), device(x, y, (z + 7) % 8, core)
    up2, down2 = device(x, y, (z + 2) % 8, core), device(x, y, (z + 6) % 8, core)
    greet(list(block.values()) + list(mirror) + [up, down, up2, down2])

    locals_ = [
        pltpu.make_async_copy(kvp.at[:, pl.ds(pl.multiple_of(g * 128, 128), 128)], kvp_out.at[z, yg, xg, j], own.at[0]),
        pltpu.make_async_copy(kvc.at[:, pl.ds(pl.multiple_of(g * 128, 128), 128)], kvc_out.at[zhi, j], own.at[1]),
        pltpu.make_async_copy(qd.at[:, pl.ds(pl.multiple_of(g * 1024, 1024), 1024)], qd_out.at[j], own.at[2]),
    ]
    for copy in locals_:
        copy.start()
    copies = {0: [], 1: [], 2: []}
    for kind in range(3):
        for d in range(1, 8):
            theirs = flip(g, d)
            if kind == 0:
                src, dst = kvp.at[:, pl.ds(pl.multiple_of(theirs * 128, 128), 128)], kvp_out.at[z, yg, xg, j]
            elif kind == 1:
                src, dst = kvc.at[:, pl.ds(pl.multiple_of(theirs * 128, 128), 128)], kvc_out.at[zhi, j]
            else:
                src, dst = qd.at[:, pl.ds(pl.multiple_of(theirs * 1024, 1024), 1024)], qd_out.at[j]
            copy = remote(src, dst, sends.at[kind, d], recvs.at[kind, d], block[d])
            copy.start()
            copies[kind].append(copy)

    locals_[0].wait()
    for copy in copies[0]:
        copy.wait()
    mirrored = [
        remote(kvp_out.at[z, yg, xg], kvp_out.at[z, yg, xg], psend.at[i], precv.at[i], mirror[i]) for i in range(3)
    ]
    for copy in mirrored:
        copy.start()
    locals_[1].wait()
    for copy in copies[1]:
        copy.wait()
    near = [
        remote(kvc_out.at[zhi], kvc_out.at[zhi], csend.at[0], crecv.at[0], up2),
        remote(kvc_out.at[zhi], kvc_out.at[zhi], csend.at[1], crecv.at[1], down2),
    ]
    for copy in mirrored:
        copy.wait()
    ring = []
    for step in range(3):
        rise, fall = (z + 8 - step) % 8, (z + step) % 8
        pair = [
            remote(kvp_out.at[rise], kvp_out.at[rise], psend.at[3 + step], precv.at[3 + step], up),
            remote(kvp_out.at[fall], kvp_out.at[fall], psend.at[7 + step], precv.at[7 + step], down),
        ]
        for copy in pair:
            copy.start()
        if step == 0:
            for copy in near:
                copy.start()
        for copy in pair:
            copy.wait()
    rise, fall = (z + 5) % 8, (z + 3) % 8
    last = [
        remote(kvp_out.at[rise, 0], kvp_out.at[rise, 0], psend.at[6], precv.at[6], up),
        remote(kvp_out.at[fall, 1], kvp_out.at[fall, 1], psend.at[10], precv.at[10], down),
    ]
    for copy in last:
        copy.start()
    for copy in near:
        copy.wait()
    below, above = (zhi + 3) % 4, (zhi + 1) % 4
    first, second = pl.ds(0, 4), pl.ds(4, 4)
    far = [
        remote(kvc_out.at[below, first], kvc_out.at[below, first], csend.at[2], crecv.at[2], up2),
        remote(kvc_out.at[above, second], kvc_out.at[above, second], csend.at[3], crecv.at[3], down2),
    ]
    for copy in far:
        copy.start()
    for copy in last + far:
        copy.wait()
    locals_[2].wait()
    for copy in copies[2]:
        copy.wait()


def nt(a, b):
    return lax.dot_general(a, b, (((1,), (1,)), ((), ())), preferred_element_type=f32)


def nn(a, b):
    return lax.dot_general(a, b, (((1,), (0,)), ((), ())), preferred_element_type=f32)


PART = 1024
PROMPT, SPAN = 2048, 512


def attend_kernel(
    meta, qd, kvp, kvc, od, dkvp, dkvc,
    kp, vp, kpt, vpt, ks, vs, kst, vst, scores, dkp, dvp, dks, dvs,
):
    z, yg, xg = meta[0], meta[1], meta[2]
    zhi = z // 2

    for i in range(8):
        both = kvp[i].reshape(32, 16, 128).astype(f32)
        rows = slice(i * 256, (i + 1) * 256)
        keys = both[:, 0:8, :].reshape(256, 128)
        values = both[:, 8:16, :].reshape(256, 128)
        kp[rows, :] = keys.astype(bf16)
        vp[rows, :] = values.astype(bf16)
        kpt[:, rows] = keys.T.astype(bf16)
        vpt[:, rows] = values.T.astype(bf16)
    for s in range(2):
        for half in range(2):
            for hi in range(4):
                for c in range(2):
                    at = half * 256 + hi * 64 + c * 32
                    ks[s, at : at + 32, :] = kvc[hi, s * 4 + half * 2 + c, 0:32, :]
                    vs[s, at : at + 32, :] = kvc[hi, s * 4 + half * 2 + c, 32:64, :]
        kst[s] = ks[s].astype(f32).T.astype(bf16)
        vst[s] = vs[s].astype(f32).T.astype(bf16)
    dkp[...] = jnp.zeros_like(dkp)
    dvp[...] = jnp.zeros_like(dvp)
    dks[...] = jnp.zeros_like(dks)
    dvs[...] = jnp.zeros_like(dvs)

    def tile(queries, grads, cand, row_at, live):
        peak = jnp.full((8, 256), HIDDEN, f32)
        for c in range(PROMPT // PART):
            rows = slice(c * PART, (c + 1) * PART)
            s = nt(kp[rows, :], queries)
            if not cand:
                n = c * PART + lax.broadcasted_iota(jnp.int32, (PART, 1), 0)
                zz = n // 256
                key_at = (
                    (zz % 2) * 1024 + (zz // 2) * 16
                    + ((n // 128) % 2) * 512 + ((n // 32) % 2) * 256
                    + ((n // 64) % 2) * 128 + ((n // 16) % 2) * 64
                    + ((n // 8) % 2) * 8 + n % 8
                )
                s = jnp.where(key_at <= row_at, s, HIDDEN)
            scores[rows, :] = s
            peak = jnp.maximum(peak, jnp.max(s.reshape(PART // 8, 8, 256), axis=0))
        parts = [slice(c * PART, (c + 1) * PART) for c in range(PROMPT // PART)]
        if cand:
            spans = []
            for i in range(2):
                lanes = slice(i * 128, (i + 1) * 128)
                s = nt(ks[i], queries[lanes, :])
                t = lax.broadcasted_iota(jnp.int32, (SPAN, 1), 0)
                s = jnp.where(t <= row_at[:, lanes], s, HIDDEN)
                scores[PROMPT:, lanes] = s
                spans.append(jnp.max(s.reshape(SPAN // 8, 8, 128), axis=0))
            peak = jnp.maximum(peak, jnp.concatenate(spans, axis=1))
            parts.append(slice(PROMPT, PROMPT + SPAN))
        peak = jnp.max(peak, axis=0, keepdims=True)
        total = jnp.zeros((8, 256), f32)
        for rows in parts:
            e = jnp.exp2((scores[rows, :] - peak) * SCALE2)
            scores[rows, :] = e
            total = total + jnp.sum(e.reshape(-1, 8, 256), axis=0)
        share = 1.0 / jnp.sum(total, axis=0, keepdims=True)
        out = jnp.zeros((128, 256), f32)
        for rows in parts[: PROMPT // PART]:
            half = (scores[rows, :] * share).astype(bf16)
            out = out + nn(vpt[:, rows], half)
            dvp[rows, :] += nn(half, grads)
        if cand:
            half = (scores[PROMPT:, :] * share).astype(bf16)
            spans = []
            for i in range(2):
                lanes = slice(i * 128, (i + 1) * 128)
                spans.append(nn(vst[i], half[:, lanes]))
                dvs[i] += nn(half[:, lanes], grads[lanes, :])
            out = out + jnp.concatenate(spans, axis=1)
            out = jnp.where(live, out, 0.0)
        delta = jnp.sum(out * grads.astype(f32).T, axis=0, keepdims=True)
        dq = jnp.zeros((128, 256), f32)
        for rows in parts[: PROMPT // PART]:
            dw = nt(vp[rows, :], grads)
            ds = (scores[rows, :] * share * (dw - delta)).astype(bf16)
            dq = dq + nn(kpt[:, rows], ds)
            dkp[rows, :] += nn(ds, queries)
        if cand:
            spans = []
            for i in range(2):
                lanes = slice(i * 128, (i + 1) * 128)
                dw = nt(vs[i], grads[lanes, :])
                ds = (scores[PROMPT:, lanes] * share[:, lanes] * (dw - delta[:, lanes])).astype(bf16)
                spans.append(nn(kst[i], ds))
                dks[i] += nn(ds, queries[lanes, :])
            dq = dq + jnp.concatenate(spans, axis=1)
        return out.T, (dq * SCALE).T

    lane = lax.broadcasted_iota(jnp.int32, (1, 256), 1)
    cand_at = ((lane // 64) % 2) * 256 + zhi * 64 + lane % 64
    live = cand_at < jnp.where(lane < 128, meta[3], meta[4])
    live_rows = [
        (half * 256 + zhi * 64 + lax.broadcasted_iota(jnp.int32, (64, 1), 0)) < meta[3 + s]
        for s in range(2)
        for half in range(2)
    ]
    live_rows = jnp.concatenate([m.astype(f32) for m in live_rows], axis=0) > 0.5

    def cand_head(h, carry):
        cols = pl.ds(pl.multiple_of(h * 128, 128), 128)
        queries = jnp.concatenate([qd[i, 0:32, cols] for i in range(8)], axis=0)
        grads = jnp.concatenate([qd[i, 32:64, cols] for i in range(8)], axis=0)
        grads = jnp.where(live_rows, grads.astype(f32), 0.0).astype(bf16)
        out, dq = tile(queries, grads, True, cand_at, live)
        for i in range(8):
            od[i, 0:32, cols] = out[i * 32 : (i + 1) * 32, :].astype(bf16)
            od[i, 32:64, cols] = dq[i * 32 : (i + 1) * 32, :].astype(bf16)
        return carry

    lax.fori_loop(0, 8, cand_head, 0)

    prompt_at = (
        (z % 2) * 1024 + (z // 2) * 16 + yg * 512 + xg * 128
        + ((lane // 32) % 2) * 256 + ((lane // 16) % 2) * 64 + ((lane // 8) % 2) * 8 + lane % 8
    )

    def prompt_heads(t, carry):
        queries, grads = [], []
        for h in range(4):
            cols = pl.ds(pl.multiple_of(t * 512 + h * 128, 128), 128)
            for i in range(8):
                both = qd[i, 64:80, cols].astype(f32)
                queries.append(both[0:8])
                grads.append(both[8:16])
        queries = jnp.concatenate(queries, axis=0).astype(bf16)
        grads = jnp.concatenate(grads, axis=0).astype(bf16)
        out, dq = tile(queries, grads, False, prompt_at, None)
        for h in range(4):
            cols = pl.ds(pl.multiple_of(t * 512 + h * 128, 128), 128)
            for i in range(8):
                at = h * 64 + i * 8
                both = jnp.concatenate([out[at : at + 8], dq[at : at + 8]], axis=0)
                od[i, 64:80, cols] = both.astype(bf16)
        return carry

    lax.fori_loop(0, 2, prompt_heads, 0)

    for i in range(8):
        rows = slice(i * 256, (i + 1) * 256)
        both = jnp.concatenate(
            [(dkp[rows, :] * SCALE).reshape(32, 8, 128), dvp[rows, :].reshape(32, 8, 128)], axis=1
        )
        dkvp[i] = both.astype(bf16).reshape(2, 2, 8, 16, 128)
    for s in range(2):
        for half in range(2):
            for hi in range(4):
                for c in range(2):
                    at = half * 256 + hi * 64 + c * 32
                    place = s * 4 + half * 2 + c
                    dkvc[hi, place, 0:32, :] = (dks[s, at : at + 32, :] * SCALE).astype(bf16)
                    dkvc[hi, place, 32:64, :] = dvs[s, at : at + 32, :].astype(bf16)


def scatter_kernel(
    od, dkvp, dkvc, od_out, kvp_out, kvc_out,
    rising, falling, rise_sum, fall_sum, zsum, mirrored_in, psum, cand_in, csum,
    own, sends, recvs, psend, precv, csend, crecv,
):
    x, y, z, core = coords()
    xg, yg, j, g = roles(x, y, core)
    zhi = z // 2
    block = {d: block_partner(x, y, z, core, d) for d in range(1, 8)}
    mirror = (device(3 - x, y, z, core), device(x, 3 - y, z, core), device(3 - x, 3 - y, z, core))
    up, down = device(x, y, (z + 1) % 8, core), device(x, y, (z + 7) % 8, core)
    hops = [device(x, y, (z + 2 * i) % 8, core) for i in (1, 3, 2)]
    greet(list(block.values()) + list(mirror) + [up, down] + hops)

    ring = [
        remote(dkvp.at[(z + 4) % 8, 0], rising.at[0, 0], psend.at[0], precv.at[0], up),
        remote(dkvp.at[(z + 4) % 8, 1], falling.at[0, 1], psend.at[4], precv.at[4], down),
    ]
    for copy in ring:
        copy.start()
    cand = [
        remote(dkvc.at[(zhi + i) % 4], cand_in.at[n], csend.at[n], crecv.at[n], hops[n])
        for n, i in enumerate((1, 3, 2))
    ]
    for copy in cand:
        copy.start()
    back = [pltpu.make_async_copy(od.at[j], od_out.at[:, pl.ds(pl.multiple_of(g * 1024, 1024), 1024)], own.at[0])]
    for d in range(1, 8):
        back.append(
            remote(
                od.at[flip(j, d)],
                od_out.at[:, pl.ds(pl.multiple_of(g * 1024, 1024), 1024)],
                sends.at[0, d], recvs.at[0, d], block[d],
            )
        )
    for copy in back:
        copy.start()
    for step in range(1, 4):
        for copy in ring:
            copy.wait()
        far_up, far_down = (z + 4 - step) % 8, (z + 4 + step) % 8
        if step == 1:
            rise_sum[0, 0] = (dkvp[far_up, 0].astype(f32) + rising[0, 0].astype(f32)).astype(bf16)
            rise_sum[0, 1] = dkvp[far_up, 1]
            fall_sum[0, 1] = (dkvp[far_down, 1].astype(f32) + falling[0, 1].astype(f32)).astype(bf16)
            fall_sum[0, 0] = dkvp[far_down, 0]
        else:
            rise_sum[step - 1] = (dkvp[far_up].astype(f32) + rising[step - 1].astype(f32)).astype(bf16)
            fall_sum[step - 1] = (dkvp[far_down].astype(f32) + falling[step - 1].astype(f32)).astype(bf16)
        ring = [
            remote(rise_sum.at[step - 1], rising.at[step], psend.at[step], precv.at[step], up),
            remote(fall_sum.at[step - 1], falling.at[step], psend.at[4 + step], precv.at[4 + step], down),
        ]
        for copy in ring:
            copy.start()
    for copy in cand:
        copy.wait()
    csum[...] = (
        dkvc[zhi].astype(f32) + cand_in[0].astype(f32) + cand_in[1].astype(f32) + cand_in[2].astype(f32)
    ).astype(bf16)
    cols = pl.ds(pl.multiple_of(g * 128, 128), 128)
    cand_back = [pltpu.make_async_copy(csum.at[j], kvc_out.at[:, cols], own.at[1])]
    for d in range(1, 8):
        cand_back.append(remote(csum.at[flip(j, d)], kvc_out.at[:, cols], sends.at[1, d], recvs.at[1, d], block[d]))
    for copy in cand_back:
        copy.start()
    for copy in ring:
        copy.wait()
    zsum[...] = (dkvp[z].astype(f32) + rising[3].astype(f32) + falling[3].astype(f32)).astype(bf16)
    across = [
        remote(zsum.at[yg, 1 - xg], mirrored_in.at[0], psend.at[8], precv.at[8], mirror[0]),
        remote(zsum.at[1 - yg, xg], mirrored_in.at[1], psend.at[9], precv.at[9], mirror[1]),
        remote(zsum.at[1 - yg, 1 - xg], mirrored_in.at[2], psend.at[10], precv.at[10], mirror[2]),
    ]
    for copy in across:
        copy.start()
    for copy in across:
        copy.wait()
    psum[...] = (
        zsum[yg, xg].astype(f32)
        + mirrored_in[0].astype(f32) + mirrored_in[1].astype(f32) + mirrored_in[2].astype(f32)
    ).astype(bf16)
    prompt_back = [pltpu.make_async_copy(psum.at[j], kvp_out.at[:, cols], own.at[2])]
    for d in range(1, 8):
        prompt_back.append(remote(psum.at[flip(j, d)], kvp_out.at[:, cols], sends.at[2, d], recvs.at[2, d], block[d]))
    for copy in prompt_back:
        copy.start()
    for copy in back + cand_back + prompt_back:
        copy.wait()


ANY = pl.BlockSpec(memory_space=pl.ANY)
VMEM = pl.BlockSpec(memory_space=pltpu.VMEM)
SMEM = pl.BlockSpec(memory_space=pltpu.SMEM)


def local(
    prompt_q, prompt_k, prompt_v, prompt_dout, cand_q, cand_k, cand_v, cand_dout, cand_len, placement
):
    x, y, z, core = coords()
    slots = (z % 2) * 8 + ((y // 2) * 2 + jnp.arange(2, dtype=jnp.int32)) * 2 + x // 2
    lengths = jnp.sum(jnp.where(placement[None, :] == slots[:, None], cand_len[None, :], 0), axis=1)
    meta = jnp.concatenate([jnp.stack([z, y // 2, x // 2]), lengths]).astype(jnp.int32)
    qd = jnp.concatenate([cand_q, cand_dout, prompt_q, prompt_dout], axis=0)
    kvp = jnp.concatenate([prompt_k, prompt_v], axis=0)
    kvc = jnp.concatenate([cand_k, cand_v], axis=0)
    DMA = pltpu.SemaphoreType.DMA
    qd_shape = jax.ShapeDtypeStruct((8, 80, 1024), bf16)
    kvp_shape = jax.ShapeDtypeStruct((8, 2, 2, 8, 16, 128), bf16)
    kvc_shape = jax.ShapeDtypeStruct((4, 8, 64, 128), bf16)
    qd, kvp, kvc = pl.pallas_call(
        gather_kernel,
        out_shape=(qd_shape, kvp_shape, kvc_shape),
        in_specs=[ANY] * 3,
        out_specs=(ANY,) * 3,
        scratch_shapes=[DMA((3,)), DMA((3, 8)), DMA((3, 8)), DMA((11,)), DMA((11,)), DMA((4,)), DMA((4,))],
        compiler_params=pltpu.CompilerParams(collective_id=0, has_side_effects=True),
        name="gather",
    )(qd, kvp, kvc)
    od, dkvp, dkvc = pl.pallas_call(
        attend_kernel,
        out_shape=(qd_shape, kvp_shape, kvc_shape),
        in_specs=[SMEM, VMEM, VMEM, VMEM],
        out_specs=(VMEM,) * 3,
        scratch_shapes=[
            pltpu.VMEM((PROMPT, 128), bf16), pltpu.VMEM((PROMPT, 128), bf16),
            pltpu.VMEM((128, PROMPT), bf16), pltpu.VMEM((128, PROMPT), bf16),
            pltpu.VMEM((2, SPAN, 128), bf16), pltpu.VMEM((2, SPAN, 128), bf16),
            pltpu.VMEM((2, 128, SPAN), bf16), pltpu.VMEM((2, 128, SPAN), bf16),
            pltpu.VMEM((PROMPT + SPAN, 256), f32),
            pltpu.VMEM((PROMPT, 128), f32), pltpu.VMEM((PROMPT, 128), f32),
            pltpu.VMEM((2, SPAN, 128), f32), pltpu.VMEM((2, SPAN, 128), f32),
        ],
        compiler_params=pltpu.CompilerParams(vmem_limit_bytes=48 * 2**20),
        name="attend",
    )(meta, qd, kvp, kvc)
    part = (2, 2, 8, 16, 128)
    od, dkvp, dkvc = pl.pallas_call(
        scatter_kernel,
        out_shape=(
            jax.ShapeDtypeStruct((80, 8192), bf16),
            jax.ShapeDtypeStruct((16, 1024), bf16),
            jax.ShapeDtypeStruct((64, 1024), bf16),
        ),
        in_specs=[ANY, VMEM, VMEM],
        out_specs=(ANY,) * 3,
        scratch_shapes=[
            pltpu.VMEM((4,) + part, bf16), pltpu.VMEM((4,) + part, bf16),
            pltpu.VMEM((3,) + part, bf16), pltpu.VMEM((3,) + part, bf16),
            pltpu.VMEM(part, bf16), pltpu.VMEM((3, 8, 16, 128), bf16), pltpu.VMEM((8, 16, 128), bf16),
            pltpu.VMEM((3, 8, 64, 128), bf16), pltpu.VMEM((8, 64, 128), bf16),
            DMA((3,)), DMA((3, 8)), DMA((3, 8)), DMA((11,)), DMA((11,)), DMA((3,)), DMA((3,)),
        ],
        compiler_params=pltpu.CompilerParams(
            collective_id=1, has_side_effects=True, vmem_limit_bytes=24 * 2**20
        ),
        name="scatter",
    )(od, dkvp, dkvc)
    return (
        od[64:72], od[72:80], dkvp[0:8], dkvp[8:16],
        od[0:32], od[32:64], dkvc[0:32], dkvc[32:64],
    )


def solution(mesh):
    rows = P(("seq", "head"), None)
    return jax.shard_map(
        local,
        mesh=mesh,
        in_specs=(rows,) * 8 + (P(), P()),
        out_specs=(rows,) * 8,
        check_vma=False,
    )
```

```python
import functools
import math

import jax
import jax.numpy as jnp
from jax import lax
from jax.experimental import pallas as pl
from jax.experimental.pallas import tpu as pltpu
from jax.sharding import PartitionSpec as P

HD = 128
SCALE = 1.0 / math.sqrt(HD)
SCALE2 = SCALE * math.log2(math.e)
MESH = pl.DeviceIdType.MESH
f32, bf16 = jnp.float32, jnp.bfloat16
HIDDEN = -1e30
PART = 512
PROMPT, SPAN = 2048, 512
KEYS = PROMPT + SPAN
LANES = 2560


def coords():
    seq, head = lax.axis_index("seq"), lax.axis_index("head")
    x, y = seq % 4, (seq // 4) % 4
    z = (head // 2) * 2 + seq // 16
    return x, y, z, head % 2


def device(x, y, z, core):
    return ((z % 2) * 16 + y * 4 + x, (z // 2) * 2 + core)


def roles(x, y, core):
    xg, sx, yg, sy = x // 2, x % 2, y // 2, y % 2
    j = sy * 4 + sx * 2 + core
    g = ((sy + yg) % 2) * 4 + ((sx + xg) % 2) * 2 + core
    return xg, yg, j, g


def flip(value, bits):
    out = 0
    for bit in (4, 2, 1):
        digit = (value // bit) % 2
        out = out + bit * ((1 - digit) if bits & bit else digit)
    return out


def block_partner(x, y, z, core, d):
    px = x // 2 * 2 + (1 - x % 2 if d & 2 else x % 2)
    py = y // 2 * 2 + (1 - y % 2 if d & 4 else y % 2)
    return device(px, py, z, 1 - core if d & 1 else core)


def greet(partners):
    barrier = pltpu.get_barrier_semaphore()
    for partner in partners:
        pl.semaphore_signal(barrier, inc=1, device_id=partner, device_id_type=MESH)
    pl.semaphore_wait(barrier, len(partners))


def remote(src, dst, send, recv, target):
    return pltpu.make_async_remote_copy(
        src_ref=src, dst_ref=dst, send_sem=send, recv_sem=recv, device_id=target, device_id_type=MESH
    )


def start(copies):
    for copy in copies:
        copy.start()


def wait(copies):
    for copy in copies:
        copy.wait()


def nt(a, b):
    return lax.dot_general(a, b, (((1,), (1,)), ((), ())), preferred_element_type=f32)


def nn(a, b):
    return lax.dot_general(a, b, (((1,), (0,)), ((), ())), preferred_element_type=f32)


def columns(index, width):
    return pl.ds(pl.multiple_of(index * width, width), width)


def kernel(
    cand_len, placement,
    prompt_q, prompt_k, prompt_v, prompt_dout, cand_q, cand_k, cand_v, cand_dout,
    oc_out, dqc_out, pp_out, kvp_out, ck_out, cv_out,
    pp_stage, kv_stage, kvp_in, kc, vc, qc_in, pp_in, gc_in, kq, vq,
    q_all, g_all, ks, vs, kpt, vpt, kst, vst,
    scores, halves, peaks, shares, deltas, prompt_out,
    oc, dqc, pp, dvb, dkb, rv, rk, zv, zk, zv_in, zk_in, dvown, dkown, vsum,
    dvc, dkc, cv_in, ck_in, cv_sum, ck_sum, psum,
    own, asend, arecv, zsend, zrecv, msend, mrecv, csend, crecv, bsend, brecv,
):
    x, y, z, core = coords()
    xg, yg, j, g = roles(x, y, core)
    zhi, sy = z // 2, y % 2
    block = {d: block_partner(x, y, z, core, d) for d in range(1, 8)}
    mirror = {
        1: device(3 - x, y, z, core), 2: device(x, 3 - y, z, core), 3: device(3 - x, 3 - y, z, core)
    }
    column = {d: device(x, y, (z + d) % 8, core) for d in range(1, 8)}

    both = jnp.concatenate([prompt_k[...].astype(f32), prompt_v[...].astype(f32)], axis=0)
    kv_stage[...] = both.astype(bf16)
    both = jnp.concatenate([prompt_q[...].astype(f32), prompt_dout[...].astype(f32)], axis=0)
    pp_stage[...] = both.astype(bf16)

    greet(list(block.values()) + list(mirror.values()) + list(column.values()))

    def exchange(kind, source, width, target):
        copies = [pltpu.make_async_copy(source.at[:, columns(g, width)], target, own.at[kind])]
        for d in range(1, 8):
            copies.append(
                remote(
                    source.at[:, columns(flip(g, d), width)], target,
                    asend.at[kind, d], arecv.at[kind, d], block[d],
                )
            )
        start(copies)
        return copies

    kvp_moves = exchange(0, kv_stage, 128, kvp_in.at[j])
    kc_moves = exchange(1, cand_k, 128, kc.at[zhi, j])
    q_moves = exchange(2, cand_q, 1024, qc_in.at[j])
    pp_moves = exchange(3, pp_stage, 1024, pp_in.at[j])
    vc_moves = exchange(4, cand_v, 128, vc.at[zhi, j])
    g_moves = exchange(5, cand_dout, 1024, gc_in.at[j])

    wait(kvp_moves)
    both = kvp_in[...].astype(f32)
    kq[0, z] = both[:, 0:8, :].reshape(64, 128).astype(bf16)
    vq[0, z] = both[:, 8:16, :].reshape(64, 128).astype(bf16)
    kz = [remote(kq.at[0, z], kq.at[0, z], zsend.at[0, d], zrecv.at[0, d], column[d]) for d in range(1, 8)]
    vz = [remote(vq.at[0, z], vq.at[0, z], zsend.at[1, d], zrecv.at[1, d], column[d]) for d in range(1, 8)]
    start(kz)
    wait(kc_moves)
    kc_near = [
        remote(kc.at[zhi], kc.at[zhi], csend.at[0], crecv.at[0], column[2]),
        remote(kc.at[zhi], kc.at[zhi], csend.at[1], crecv.at[1], column[6]),
    ]
    start(kc_near)
    start(vz)
    wait(kz)
    kquads = [remote(kq.at[0], kq.at[p], msend.at[0, p], mrecv.at[0, p], mirror[p]) for p in (1, 2, 3)]
    start(kquads)
    below, above = (zhi + 3) % 4, (zhi + 1) % 4
    first, second = pl.ds(0, 4), pl.ds(4, 4)
    wait(kc_near)
    kc_far = [
        remote(kc.at[below, first], kc.at[below, first], csend.at[2], crecv.at[2], column[2]),
        remote(kc.at[above, second], kc.at[above, second], csend.at[3], crecv.at[3], column[6]),
    ]
    start(kc_far)
    wait(vc_moves)
    vc_near = [
        remote(vc.at[zhi], vc.at[zhi], csend.at[4], crecv.at[4], column[2]),
        remote(vc.at[zhi], vc.at[zhi], csend.at[5], crecv.at[5], column[6]),
    ]
    start(vc_near)
    wait(vz)
    vquads = [remote(vq.at[0], vq.at[p], msend.at[1, p], mrecv.at[1, p], mirror[p]) for p in (1, 2, 3)]
    start(vquads)

    slots = (1 - sy, sy)
    wait(q_moves)
    for i in range(2):
        for k in range(4):
            rows = qc_in[slots[i] * 4 + k]
            for h in range(8):
                at = i * 1024 + h * 128 + k * 32
                q_all[at : at + 32, :] = rows[:, h * 128 : (h + 1) * 128]
    wait(pp_moves)
    for h in range(8):
        both = pp_in[:, :, h * 128 : (h + 1) * 128].astype(f32)
        at = 2048 + h * 64
        q_all[at : at + 64, :] = both[:, 0:8, :].reshape(64, 128).astype(bf16)
        g_all[at : at + 64, :] = both[:, 8:16, :].reshape(64, 128).astype(bf16)

    peaks[...] = jnp.full(peaks.shape, HIDDEN, f32)
    lane = lax.broadcasted_iota(jnp.int32, (1, 256), 1)
    cand_at = ((lane // 64) % 2) * 256 + zhi * 64 + lane % 64
    prompt_at = (
        (z % 2) * 1024 + zhi * 16 + yg * 512 + xg * 128
        + ((lane // 32) % 2) * 256 + ((lane // 16) % 2) * 64 + ((lane // 8) % 2) * 8 + lane % 8
    )

    def top(s):
        return jnp.max(s.reshape(-1, 8, 256), axis=0)

    def score_part(p):
        rows = slice(p * PART, (p + 1) * PART)
        keys = kq[p].reshape(PART, 128)

        def cand(t, carry):
            at = columns(t, 256)
            s = nt(keys, q_all[at, :])
            scores[rows, at] = s
            peaks[:, at] = jnp.maximum(peaks[:, at], top(s))
            return carry

        lax.fori_loop(0, 8, cand, 0)
        n = lax.broadcasted_iota(jnp.int32, (PART, 1), 0)
        zz = n // 64
        ygp = yg if p < 2 else 1 - yg
        xgp = xg if p % 2 == 0 else 1 - xg
        key_at = (
            (zz % 2) * 1024 + (zz // 2) * 16 + ygp * 512 + ((n // 32) % 2) * 256
            + xgp * 128 + ((n // 16) % 2) * 64 + ((n // 8) % 2) * 8 + n % 8
        )

        def prompt(t, carry):
            at = columns(t, 256)
            s = jnp.where(key_at <= prompt_at, nt(keys, q_all[at, :]), HIDDEN)
            scores[rows, at] = s
            peaks[:, at] = jnp.maximum(peaks[:, at], top(s))
            return carry

        lax.fori_loop(8, 10, prompt, 0)
        kpt[:, rows] = keys.astype(f32).T.astype(bf16)

    score_part(0)
    for p in (1, 2, 3):
        wait([kquads[p - 1]])
        score_part(p)

    def slot_rows(source, target, turned):
        for i in range(2):
            for half in range(2):
                for hi in range(4):
                    for c in range(2):
                        at = half * 256 + hi * 64 + c * 32
                        target[i, at : at + 32, :] = source[hi, slots[i] * 4 + half * 2 + c]
            turned[i] = target[i].astype(f32).T.astype(bf16)

    wait(vc_near)
    vc_far = [
        remote(vc.at[below, first], vc.at[below, first], csend.at[6], crecv.at[6], column[2]),
        remote(vc.at[above, second], vc.at[above, second], csend.at[7], crecv.at[7], column[6]),
    ]
    start(vc_far)
    wait(kc_far)
    slot_rows(kc, ks, kst)
    span_at = lax.broadcasted_iota(jnp.int32, (SPAN, 1), 0)

    def score_slot(t, carry):
        at = columns(t, 256)
        s = jnp.where(span_at <= cand_at, nt(ks[t // 4], q_all[at, :]), HIDDEN)
        scores[PROMPT:, at] = s
        peaks[:, at] = jnp.maximum(peaks[:, at], top(s))
        return carry

    lax.fori_loop(0, 8, score_slot, 0)

    lengths = []
    for i in range(2):
        slot = (z % 2) * 8 + ((y // 2) * 2 + slots[i]) * 2 + x // 2
        length = jnp.int32(0)
        for c in range(16):
            length = length + jnp.where(placement[c] == slot, cand_len[c], 0)
        lengths.append(length)
    wait(g_moves)
    row = lax.broadcasted_iota(jnp.int32, (32, 1), 0)
    for i in range(2):
        for k in range(4):
            kept = (k // 2) * 256 + zhi * 64 + (k % 2) * 32 + row < lengths[i]
            rows = jnp.where(kept, gc_in[slots[i] * 4 + k].astype(f32), 0.0).astype(bf16)
            for h in range(8):
                at = i * 1024 + h * 128 + k * 32
                g_all[at : at + 32, :] = rows[:, h * 128 : (h + 1) * 128]
    wait(vquads)
    for p in range(4):
        vpt[:, p * PART : (p + 1) * PART] = vq[p].reshape(PART, 128).astype(f32).T.astype(bf16)
    wait(vc_far)
    slot_rows(vc, vs, vst)

    def weigh(t, cand, i):
        at = columns(t, 256)
        parts = KEYS // PART if cand else PROMPT // PART
        peak = jnp.max(peaks[:, at], axis=0, keepdims=True)
        total = jnp.zeros((8, 256), f32)
        for p in range(parts):
            rows = slice(p * PART, (p + 1) * PART)
            e = jnp.exp2((scores[rows, at] - peak) * SCALE2)
            scores[rows, at] = e
            total = total + jnp.sum(e.reshape(-1, 8, 256), axis=0)
        share = 1.0 / jnp.sum(total, axis=0, keepdims=True)
        shares[:, at] = jnp.broadcast_to(share, (8, 256))
        for p in range(parts):
            rows = slice(p * PART, (p + 1) * PART)
            halves[rows, at] = (scores[rows, at] * share).astype(bf16)
        out = nn(vpt[...], halves[0:PROMPT, at])
        if cand:
            out = out + nn(vst[i], halves[PROMPT:, at])
            out = jnp.where(cand_at < lengths[i], out, 0.0)
        delta = jnp.sum(out * g_all[at, :].astype(f32).T, axis=0, keepdims=True)
        deltas[:, at] = jnp.broadcast_to(delta, (8, 256))
        return out.T

    def put_cand(target, i, pair, rows):
        for a in range(2):
            for k in range(4):
                at = a * 128 + k * 32
                target[slots[i] * 4 + k, :, columns(pair * 2 + a, 128)] = rows[at : at + 32, :].astype(bf16)

    def give_back(kind, source, target, which):
        copies = []
        if 0 in which:
            copies.append(pltpu.make_async_copy(source.at[j], target, own.at[6 + kind]))
        for d in which:
            if d:
                copies.append(remote(source.at[flip(j, d)], target, bsend.at[kind, d], brecv.at[kind, d], block[d]))
        start(copies)
        return copies

    OTHER, OWN = (4, 5, 6, 7), (1, 2, 3, 0)
    back = []
    for i, which in enumerate((OTHER, OWN)):

        def weigh_cand(pair, carry, i=i):
            put_cand(oc, i, pair, weigh(i * 4 + pair, True, i))
            return carry

        lax.fori_loop(0, 4, weigh_cand, 0)
        back += give_back(0, oc, oc_out.at[:, columns(g, 1024)], which)

    def weigh_prompt(t, carry):
        prompt_out[columns(t, 256), :] = weigh(8 + t, False, None)
        return carry

    lax.fori_loop(0, 2, weigh_prompt, 0)

    def cand_terms(sums, target, i):
        for half in range(2):
            for hi in range(4):
                for c in range(2):
                    at = half * 256 + hi * 64 + c * 32
                    target[hi, slots[i] * 4 + half * 2 + c] = sums[at : at + 32, :].astype(bf16)

    def terms(others, scale, boxes, mine, inbox, kind, cand_box, cand_inbox):
        for i in range(2):
            rows = slice(i * 1024, (i + 1) * 1024)
            cand_terms(nn(halves[PROMPT:, rows], others[rows, :]) * scale, cand_box, i)
        cand_moves = [
            remote(
                cand_box.at[(zhi + n) % 4], cand_inbox.at[n - 1],
                csend.at[8 + kind * 3 + n - 1], crecv.at[8 + kind * 3 + n - 1], column[2 * n],
            )
            for n in (1, 2, 3)
        ]
        start(cand_moves)
        moves = []
        for p in (3, 1, 2, 0):
            total = nn(halves[p * PART : (p + 1) * PART, :], others[...]) * scale
            if p:
                boxes[p - 1] = total.reshape(8, 64, 128).astype(bf16)
                moves.append(
                    remote(boxes.at[p - 1], inbox.at[p - 1], msend.at[2 + kind, p], mrecv.at[2 + kind, p], mirror[p])
                )
                start(moves[-1:])
            else:
                mine[...] = total.reshape(8, 64, 128)
        return cand_moves, moves

    def along_z(mine, inbox, moves, stage, landed, kind):
        wait(moves)
        total = mine[...] + inbox[0].astype(f32) + inbox[1].astype(f32) + inbox[2].astype(f32)
        stage[...] = total.astype(bf16)
        hops = [
            remote(stage.at[(z + d) % 8], landed.at[d - 1], zsend.at[2 + kind, d], zrecv.at[2 + kind, d], column[d])
            for d in range(1, 8)
        ]
        start(hops)
        return hops

    def final(stage, landed, hops):
        wait(hops)
        total = stage[z].astype(f32)
        for d in range(7):
            total = total + landed[d].astype(f32)
        return total

    def cand_final(box, inbox, moves, total):
        wait(moves)
        total[...] = (
            box[zhi].astype(f32) + inbox[0].astype(f32) + inbox[1].astype(f32) + inbox[2].astype(f32)
        ).astype(bf16)

    vcand_moves, v_moves = terms(g_all, 1.0, dvb, dvown, rv, 0, dvc, cv_in)

    def grade(t, cand, i):
        at = columns(t, 256)
        grads = g_all[at, :]
        share, delta = shares[0:1, at], deltas[0:1, at]
        for p in range(PROMPT // PART):
            rows = slice(p * PART, (p + 1) * PART)
            dw = nt(vq[p].reshape(PART, 128), grads)
            halves[rows, at] = (scores[rows, at] * share * (dw - delta)).astype(bf16)
        dq = nn(kpt[...], halves[0:PROMPT, at])
        if cand:
            dw = nt(vs[i], grads)
            halves[PROMPT:, at] = (scores[PROMPT:, at] * share * (dw - delta)).astype(bf16)
            dq = dq + nn(kst[i], halves[PROMPT:, at])
        return (dq * SCALE).T

    def grade_prompt(t, carry):
        dq = grade(8 + t, False, None)
        out = prompt_out[columns(t, 256), :]
        for h in range(4):
            rows = slice(h * 64, (h + 1) * 64)
            both = jnp.concatenate([out[rows].reshape(8, 8, 128), dq[rows].reshape(8, 8, 128)], axis=1)
            pp[:, :, columns(t * 4 + h, 128)] = both.astype(bf16)
        return carry

    lax.fori_loop(0, 2, grade_prompt, 0)
    back += give_back(1, pp, pp_out.at[:, columns(g, 1024)], OTHER + OWN)
    for i, which in enumerate((OTHER, OWN)):

        def grade_cand(pair, carry, i=i):
            put_cand(dqc, i, pair, grade(i * 4 + pair, True, i))
            return carry

        lax.fori_loop(0, 4, grade_cand, 0)
        back += give_back(2, dqc, dqc_out.at[:, columns(g, 1024)], which)
        if i == 0:
            v_hops = along_z(dvown, rv, v_moves, zv, zv_in, 0)
            cand_final(dvc, cv_in, vcand_moves, cv_sum)
            back += give_back(3, cv_sum, cv_out.at[:, columns(g, 128)], OTHER + OWN)

    kcand_moves, k_moves = terms(q_all, SCALE, dkb, dkown, rk, 1, dkc, ck_in)
    k_hops = along_z(dkown, rk, k_moves, zk, zk_in, 1)
    vsum[...] = final(zv, zv_in, v_hops)
    cand_final(dkc, ck_in, kcand_moves, ck_sum)
    back += give_back(4, ck_sum, ck_out.at[:, columns(g, 128)], OTHER + OWN)
    ksum = final(zk, zk_in, k_hops)
    both = jnp.concatenate([ksum.reshape(8, 8, 128), vsum[...].reshape(8, 8, 128)], axis=1)
    psum[...] = both.astype(bf16)
    back += give_back(5, psum, kvp_out.at[:, columns(g, 128)], OTHER + OWN)
    wait(back)


ANY = pl.BlockSpec(memory_space=pl.ANY)
VMEM = pl.BlockSpec(memory_space=pltpu.VMEM)
SMEM = pl.BlockSpec(memory_space=pltpu.SMEM)


def local(
    prompt_q, prompt_k, prompt_v, prompt_dout, cand_q, cand_k, cand_v, cand_dout, cand_len, placement
):
    DMA = pltpu.SemaphoreType.DMA

    def half(*shape):
        return pltpu.VMEM(shape, bf16)

    def full(*shape):
        return pltpu.VMEM(shape, f32)

    def result(*shape):
        return jax.ShapeDtypeStruct(shape, bf16)

    oc, dqc, pp, kvp, ck, cv = pl.pallas_call(
        kernel,
        out_shape=(
            result(32, 8192), result(32, 8192), result(16, 8192), result(16, 1024), result(32, 1024), result(32, 1024)
        ),
        in_specs=[SMEM] * 2 + [VMEM] * 4 + [ANY] * 4,
        out_specs=(ANY,) * 6,
        scratch_shapes=[
            half(16, 8192), half(16, 1024), half(8, 16, 128), half(4, 8, 32, 128), half(4, 8, 32, 128),
            half(8, 32, 1024), half(8, 16, 1024), half(8, 32, 1024), half(4, 8, 64, 128), half(4, 8, 64, 128),
            half(LANES, 128), half(LANES, 128), half(2, SPAN, 128), half(2, SPAN, 128),
            half(128, PROMPT), half(128, PROMPT), half(2, 128, SPAN), half(2, 128, SPAN),
            full(KEYS, LANES), half(KEYS, LANES), full(8, LANES), full(8, LANES), full(8, LANES), full(512, 128),
            half(8, 32, 1024), half(8, 32, 1024), half(8, 16, 1024),
            half(3, 8, 64, 128), half(3, 8, 64, 128), half(3, 8, 64, 128), half(3, 8, 64, 128),
            half(8, 64, 128), half(8, 64, 128), half(7, 64, 128), half(7, 64, 128),
            full(8, 64, 128), full(8, 64, 128), full(64, 128),
            half(4, 8, 32, 128), half(4, 8, 32, 128), half(3, 8, 32, 128), half(3, 8, 32, 128),
            half(8, 32, 128), half(8, 32, 128), half(8, 16, 128),
            DMA((12,)), DMA((6, 8)), DMA((6, 8)), DMA((4, 8)), DMA((4, 8)), DMA((4, 4)), DMA((4, 4)),
            DMA((14,)), DMA((14,)), DMA((6, 8)), DMA((6, 8)),
        ],
        compiler_params=pltpu.CompilerParams(
            collective_id=0, has_side_effects=True, vmem_limit_bytes=56 * 2**20
        ),
        name="layer",
    )(
        cand_len, placement,
        prompt_q, prompt_k, prompt_v, prompt_dout, cand_q, cand_k, cand_v, cand_dout,
    )
    return (pp[0:8], pp[8:16], kvp[0:8], kvp[8:16], oc, dqc, ck, cv)


def solution(mesh):
    rows = P(("seq", "head"), None)
    return jax.shard_map(
        local,
        mesh=mesh,
        in_specs=(rows,) * 8 + (P(), P()),
        out_specs=(rows,) * 8,
        check_vma=False,
    )
```

```python
import functools
import math

import jax
import jax.numpy as jnp
from jax import lax
from jax.experimental import pallas as pl
from jax.experimental.pallas import tpu as pltpu
from jax.sharding import PartitionSpec as P

HD = 128
SCALE = 1.0 / math.sqrt(HD)
SCALE2 = SCALE * math.log2(math.e)
MESH = pl.DeviceIdType.MESH
f32, bf16 = jnp.float32, jnp.bfloat16
HIDDEN = -1e30
PART = 512
PROMPT, SPAN = 2048, 512
KEYS = PROMPT + SPAN
LANES = 2560
WIDE = 512


def coords():
    seq, head = lax.axis_index("seq"), lax.axis_index("head")
    x, y = seq % 4, (seq // 4) % 4
    z = (head // 2) * 2 + seq // 16
    return x, y, z, head % 2


def device(x, y, z, core):
    return ((z % 2) * 16 + y * 4 + x, (z // 2) * 2 + core)


def roles(x, y, core):
    xg, sx, yg, sy = x // 2, x % 2, y // 2, y % 2
    j = sy * 4 + sx * 2 + core
    g = ((sy + yg) % 2) * 4 + ((sx + xg) % 2) * 2 + core
    return xg, yg, j, g


def flip(value, bits):
    out = 0
    for bit in (4, 2, 1):
        digit = (value // bit) % 2
        out = out + bit * ((1 - digit) if bits & bit else digit)
    return out


def block_partner(x, y, z, core, d):
    px = x // 2 * 2 + (1 - x % 2 if d & 2 else x % 2)
    py = y // 2 * 2 + (1 - y % 2 if d & 4 else y % 2)
    return device(px, py, z, 1 - core if d & 1 else core)


def greet(partners):
    barrier = pltpu.get_barrier_semaphore()
    for partner in partners:
        pl.semaphore_signal(barrier, inc=1, device_id=partner, device_id_type=MESH)
    pl.semaphore_wait(barrier, len(partners))


def remote(src, dst, send, recv, target):
    return pltpu.make_async_remote_copy(
        src_ref=src, dst_ref=dst, send_sem=send, recv_sem=recv, device_id=target, device_id_type=MESH
    )


def start(copies):
    for copy in copies:
        copy.start()


def wait(copies):
    for copy in copies:
        copy.wait()


def nt(a, b):
    return lax.dot_general(a, b, (((1,), (1,)), ((), ())), preferred_element_type=f32)


def nn(a, b):
    return lax.dot_general(a, b, (((1,), (0,)), ((), ())), preferred_element_type=f32)


def columns(index, width):
    return pl.ds(pl.multiple_of(index * width, width), width)


def kernel(
    cand_len, placement,
    prompt_q, prompt_k, prompt_v, prompt_dout, cand_q, cand_k, cand_v, cand_dout,
    oc_out, dqc_out, pp_out, kvp_out, ck_out, cv_out,
    pp_stage, kv_stage, kvp_in, kc, vc, qc_in, pp_in, gc_in, kq, vq,
    q_all, g_all, ks, vs, kpt, vpt, kst, vst,
    scores, halves, peaks, shares, deltas, prompt_out, dq,
    oc, dqc, pp, dvb, dkb, rv, rk, zv, zk, zv_in, zk_in, dvown, dkown, vsum,
    dvc, dkc, cv_in, ck_in, cv_sum, ck_sum, psum,
    own, asend, arecv, zsend, zrecv, msend, mrecv, csend, crecv, bsend, brecv,
):
    x, y, z, core = coords()
    xg, yg, j, g = roles(x, y, core)
    zhi, sy = z // 2, y % 2
    block = {d: block_partner(x, y, z, core, d) for d in range(1, 8)}
    mirror = {
        1: device(3 - x, y, z, core), 2: device(x, 3 - y, z, core), 3: device(3 - x, 3 - y, z, core)
    }
    column = {d: device(x, y, (z + d) % 8, core) for d in range(1, 8)}

    both = jnp.concatenate([prompt_k[...].astype(f32), prompt_v[...].astype(f32)], axis=0)
    kv_stage[...] = both.astype(bf16)
    both = jnp.concatenate([prompt_q[...].astype(f32), prompt_dout[...].astype(f32)], axis=0)
    pp_stage[...] = both.astype(bf16)

    greet(list(block.values()) + list(mirror.values()) + list(column.values()))

    def exchange(kind, source, width, target):
        copies = [pltpu.make_async_copy(source.at[:, columns(g, width)], target, own.at[kind])]
        for d in range(1, 8):
            copies.append(
                remote(
                    source.at[:, columns(flip(g, d), width)], target,
                    asend.at[kind, d], arecv.at[kind, d], block[d],
                )
            )
        start(copies)
        return copies

    kvp_moves = exchange(0, kv_stage, 128, kvp_in.at[j])
    kc_moves = exchange(1, cand_k, 128, kc.at[zhi, j])
    q_moves = exchange(2, cand_q, 1024, qc_in.at[j])
    pp_moves = exchange(3, pp_stage, 1024, pp_in.at[j])
    vc_moves = exchange(4, cand_v, 128, vc.at[zhi, j])
    g_moves = exchange(5, cand_dout, 1024, gc_in.at[j])

    wait(kvp_moves)
    both = kvp_in[...].astype(f32)
    kq[0, z] = both[:, 0:8, :].reshape(64, 128).astype(bf16)
    vq[0, z] = both[:, 8:16, :].reshape(64, 128).astype(bf16)
    NEAREST = (1, 7, 2, 6, 3, 5, 4)

    def along_z_in(which, kind):
        moves = {
            d: remote(which.at[0, z], which.at[0, z], zsend.at[kind, d], zrecv.at[kind, d], column[d]) for d in NEAREST
        }
        start(moves.values())
        return moves

    def forward(which, kind, d):
        origin = (z + 8 - d) % 8
        copies = [
            remote(
                which.at[0, origin], which.at[p, origin],
                msend.at[kind, p, d], mrecv.at[kind, p, d], mirror[p],
            )
            for p in (1, 2, 3)
        ]
        start(copies)
        return copies

    kz = along_z_in(kq, 0)
    kquads = [forward(kq, 0, 0)]
    wait(kc_moves)
    kc_near = [
        remote(kc.at[zhi], kc.at[zhi], csend.at[0], crecv.at[0], column[2]),
        remote(kc.at[zhi], kc.at[zhi], csend.at[1], crecv.at[1], column[6]),
    ]
    start(kc_near)
    for d in NEAREST:
        wait([kz[d]])
        kquads.append(forward(kq, 0, d))
    vz = along_z_in(vq, 1)
    vquads = [forward(vq, 1, 0)]
    wait(vc_moves)
    vc_near = [
        remote(vc.at[zhi], vc.at[zhi], csend.at[4], crecv.at[4], column[2]),
        remote(vc.at[zhi], vc.at[zhi], csend.at[5], crecv.at[5], column[6]),
    ]
    start(vc_near)
    below, above = (zhi + 3) % 4, (zhi + 1) % 4
    first, second = pl.ds(0, 4), pl.ds(4, 4)
    wait(kc_near)
    kc_far = [
        remote(kc.at[below, first], kc.at[below, first], csend.at[2], crecv.at[2], column[2]),
        remote(kc.at[above, second], kc.at[above, second], csend.at[3], crecv.at[3], column[6]),
    ]
    start(kc_far)
    for d in NEAREST:
        wait([vz[d]])
        vquads.append(forward(vq, 1, d))

    slots = (1 - sy, sy)
    wait(q_moves)
    for i in range(2):
        for k in range(4):
            rows = qc_in[slots[i] * 4 + k]
            for h in range(8):
                at = i * 1024 + h * 128 + k * 32
                q_all[at : at + 32, :] = rows[:, h * 128 : (h + 1) * 128]
    wait(pp_moves)
    for h in range(8):
        both = pp_in[:, :, h * 128 : (h + 1) * 128].astype(f32)
        at = 2048 + h * 64
        q_all[at : at + 64, :] = both[:, 0:8, :].reshape(64, 128).astype(bf16)
        g_all[at : at + 64, :] = both[:, 8:16, :].reshape(64, 128).astype(bf16)

    peaks[...] = jnp.full(peaks.shape, HIDDEN, f32)
    lane = lax.broadcasted_iota(jnp.int32, (1, WIDE), 1)
    cand_at = ((lane // 64) % 2) * 256 + zhi * 64 + lane % 64
    prompt_at = (
        (z % 2) * 1024 + zhi * 16 + yg * 512 + xg * 128
        + ((lane // 32) % 2) * 256 + ((lane // 16) % 2) * 64 + ((lane // 8) % 2) * 8 + lane % 8
    )

    def top(s):
        return jnp.max(s.reshape(-1, 8, WIDE), axis=0)

    def score_part(p):
        rows = slice(p * PART, (p + 1) * PART)
        keys = kq[p].reshape(PART, 128)

        def cand(t, carry):
            at = columns(t, WIDE)
            s = nt(keys, q_all[at, :])
            scores[rows, at] = s
            peaks[:, at] = jnp.maximum(peaks[:, at], top(s))
            return carry

        lax.fori_loop(0, 4, cand, 0, unroll=2)
        n = lax.broadcasted_iota(jnp.int32, (PART, 1), 0)
        zz = n // 64
        ygp = yg if p < 2 else 1 - yg
        xgp = xg if p % 2 == 0 else 1 - xg
        key_at = (
            (zz % 2) * 1024 + (zz // 2) * 16 + ygp * 512 + ((n // 32) % 2) * 256
            + xgp * 128 + ((n // 16) % 2) * 64 + ((n // 8) % 2) * 8 + n % 8
        )

        s = jnp.where(key_at <= prompt_at, nt(keys, q_all[2048:, :]), HIDDEN)
        scores[rows, 2048:] = s
        peaks[:, 2048:] = jnp.maximum(peaks[:, 2048:], top(s))
        kpt[:, rows] = keys.astype(f32).T.astype(bf16)

    score_part(0)
    for p in (1, 2, 3):
        wait([copies[p - 1] for copies in kquads])
        score_part(p)

    def slot_rows(source, target, turned):
        for i in range(2):
            for half in range(2):
                for hi in range(4):
                    for c in range(2):
                        at = half * 256 + hi * 64 + c * 32
                        target[i, at : at + 32, :] = source[hi, slots[i] * 4 + half * 2 + c]
            turned[i] = target[i].astype(f32).T.astype(bf16)

    wait(vc_near)
    vc_far = [
        remote(vc.at[below, first], vc.at[below, first], csend.at[6], crecv.at[6], column[2]),
        remote(vc.at[above, second], vc.at[above, second], csend.at[7], crecv.at[7], column[6]),
    ]
    start(vc_far)
    wait(kc_far)
    slot_rows(kc, ks, kst)
    span_at = lax.broadcasted_iota(jnp.int32, (SPAN, 1), 0)

    def score_slot(t, carry):
        at = columns(t, WIDE)
        s = jnp.where(span_at <= cand_at, nt(ks[t // 2], q_all[at, :]), HIDDEN)
        scores[PROMPT:, at] = s
        peaks[:, at] = jnp.maximum(peaks[:, at], top(s))
        return carry

    lax.fori_loop(0, 4, score_slot, 0, unroll=2)

    lengths = []
    for i in range(2):
        slot = (z % 2) * 8 + ((y // 2) * 2 + slots[i]) * 2 + x // 2
        length = jnp.int32(0)
        for c in range(16):
            length = length + jnp.where(placement[c] == slot, cand_len[c], 0)
        lengths.append(length)
    wait(g_moves)
    row = lax.broadcasted_iota(jnp.int32, (32, 1), 0)
    for i in range(2):
        for k in range(4):
            kept = (k // 2) * 256 + zhi * 64 + (k % 2) * 32 + row < lengths[i]
            rows = jnp.where(kept, gc_in[slots[i] * 4 + k].astype(f32), 0.0).astype(bf16)
            for h in range(8):
                at = i * 1024 + h * 128 + k * 32
                g_all[at : at + 32, :] = rows[:, h * 128 : (h + 1) * 128]
    for copies in vquads:
        wait(copies)
    for p in range(4):
        vpt[:, p * PART : (p + 1) * PART] = vq[p].reshape(PART, 128).astype(f32).T.astype(bf16)
    wait(vc_far)
    slot_rows(vc, vs, vst)

    def weigh(t, cand, i):
        at = columns(t, 256)
        parts = KEYS // PART if cand else PROMPT // PART
        peak = jnp.max(peaks[:, at], axis=0, keepdims=True)
        total = jnp.zeros((8, 256), f32)
        for p in range(parts):
            rows = slice(p * PART, (p + 1) * PART)
            e = jnp.exp2((scores[rows, at] - peak) * SCALE2)
            scores[rows, at] = e
            total = total + jnp.sum(e.reshape(-1, 8, 256), axis=0)
        share = 1.0 / jnp.sum(total, axis=0, keepdims=True)
        shares[:, at] = jnp.broadcast_to(share, (8, 256))
        for p in range(parts):
            rows = slice(p * PART, (p + 1) * PART)
            halves[rows, at] = (scores[rows, at] * share).astype(bf16)
        out = nn(vpt[...], halves[0:PROMPT, at])
        if cand:
            out = out + nn(vst[i], halves[PROMPT:, at])
            out = jnp.where(cand_at[:, 0:256] < lengths[i], out, 0.0)
        delta = jnp.sum(out * g_all[at, :].astype(f32).T, axis=0, keepdims=True)
        deltas[:, at] = jnp.broadcast_to(delta, (8, 256))
        return out.T

    def put_cand(target, i, pair, rows):
        for a in range(2):
            for k in range(4):
                at = a * 128 + k * 32
                target[slots[i] * 4 + k, :, columns(pair * 2 + a, 128)] = rows[at : at + 32, :].astype(bf16)

    def give_back(kind, source, target, which):
        copies = []
        if 0 in which:
            copies.append(pltpu.make_async_copy(source.at[j], target, own.at[6 + kind]))
        for d in which:
            if d:
                copies.append(remote(source.at[flip(j, d)], target, bsend.at[kind, d], brecv.at[kind, d], block[d]))
        start(copies)
        return copies

    OTHER, OWN = (4, 5, 6, 7), (1, 2, 3, 0)
    back = []
    for i, which in enumerate((OTHER, OWN)):

        def weigh_cand(pair, carry, i=i):
            put_cand(oc, i, pair, weigh(i * 4 + pair, True, i))
            return carry

        lax.fori_loop(0, 4, weigh_cand, 0, unroll=2)
        back += give_back(0, oc, oc_out.at[:, columns(g, 1024)], which)

    def weigh_prompt(t, carry):
        prompt_out[columns(t, 256), :] = weigh(8 + t, False, None)
        return carry

    lax.fori_loop(0, 2, weigh_prompt, 0, unroll=2)

    def cand_terms(sums, target, i):
        for half in range(2):
            for hi in range(4):
                for c in range(2):
                    at = half * 256 + hi * 64 + c * 32
                    target[hi, slots[i] * 4 + half * 2 + c] = sums[at : at + 32, :].astype(bf16)

    def slot_terms(others, scale, box, inbox, kind):
        for i in range(2):
            rows = slice(i * 1024, (i + 1) * 1024)
            cand_terms(nn(halves[PROMPT:, rows], others[rows, :]) * scale, box, i)
        moves = [
            remote(
                box.at[(zhi + n) % 4], inbox.at[n - 1],
                csend.at[8 + kind * 3 + n - 1], crecv.at[8 + kind * 3 + n - 1], column[2 * n],
            )
            for n in (1, 2, 3)
        ]
        start(moves)
        return moves

    def terms(others, scale, boxes, mine, inbox, kind, p):
        total = nn(halves[p * PART : (p + 1) * PART, :], others[...]) * scale
        if p == 0:
            mine[...] = total.reshape(8, 64, 128)
            return []
        boxes[p - 1] = total.reshape(8, 64, 128).astype(bf16)
        moves = [
            remote(boxes.at[p - 1], inbox.at[p - 1], msend.at[2 + kind, p, 0], mrecv.at[2 + kind, p, 0], mirror[p])
        ]
        start(moves)
        return moves

    def along_z(mine, inbox, moves, stage, landed, kind):
        wait(moves)
        total = mine[...] + inbox[0].astype(f32) + inbox[1].astype(f32) + inbox[2].astype(f32)
        stage[...] = total.astype(bf16)
        hops = [
            remote(stage.at[(z + d) % 8], landed.at[d - 1], zsend.at[2 + kind, d], zrecv.at[2 + kind, d], column[d])
            for d in range(1, 8)
        ]
        start(hops)
        return hops

    def final(stage, landed, hops):
        wait(hops)
        total = stage[z].astype(f32)
        for d in range(7):
            total = total + landed[d].astype(f32)
        return total

    def cand_final(box, inbox, moves, total):
        wait(moves)
        total[...] = (
            box[zhi].astype(f32) + inbox[0].astype(f32) + inbox[1].astype(f32) + inbox[2].astype(f32)
        ).astype(bf16)

    FARTHEST = (3, 1, 2, 0)
    vcand_moves = slot_terms(g_all, 1.0, dvc, cv_in, 0)
    v_moves = []
    for p in FARTHEST:
        v_moves += terms(g_all, 1.0, dvb, dvown, rv, 0, p)

    def grade(values, turned, rows, at):
        dw = nt(values, g_all[at, :])
        ds = (scores[rows, at] * shares[0:1, at] * (dw - deltas[0:1, at])).astype(bf16)
        halves[rows, at] = ds
        return nn(turned, ds)

    def grade_slot(t, carry):
        at = columns(t, WIDE)
        dq[:, at] = grade(vs[t // 2], kst[t // 2], slice(PROMPT, KEYS), at)
        return carry

    lax.fori_loop(0, 4, grade_slot, 0, unroll=2)
    dq[:, 2048:] = jnp.zeros((128, WIDE), f32)
    kcand_moves = slot_terms(q_all, SCALE, dkc, ck_in, 1)

    def grade_part(p, first, last):
        rows = slice(p * PART, (p + 1) * PART)

        def body(t, carry):
            at = columns(t, WIDE)
            dq[:, at] += grade(vq[p].reshape(PART, 128), kpt[:, rows], rows, at)
            return carry

        lax.fori_loop(first, last, body, 0, unroll=2)

    k_moves = []
    for n, p in enumerate(FARTHEST[:3]):
        grade_part(p, 0, 5)
        k_moves += terms(q_all, SCALE, dkb, dkown, rk, 1, p)
        if n == 0:
            v_hops = along_z(dvown, rv, v_moves, zv, zv_in, 0)
            cand_final(dvc, cv_in, vcand_moves, cv_sum)
            back += give_back(3, cv_sum, cv_out.at[:, columns(g, 128)], OTHER + OWN)
    vsum[...] = final(zv, zv_in, v_hops)
    for i, which in enumerate((OTHER, OWN)):
        grade_part(0, i * 2, i * 2 + 2)
        for pair in range(4):
            t = i * 4 + pair
            put_cand(dqc, i, pair, (dq[:, t * 256 : (t + 1) * 256] * SCALE).T)
        back += give_back(2, dqc, dqc_out.at[:, columns(g, 1024)], which)
    grade_part(0, 4, 5)
    terms(q_all, SCALE, dkb, dkown, rk, 1, 0)
    k_hops = along_z(dkown, rk, k_moves, zk, zk_in, 1)
    for t in range(2):
        out = prompt_out[t * 256 : (t + 1) * 256, :]
        grads = (dq[:, 2048 + t * 256 : 2304 + t * 256] * SCALE).T
        for h in range(4):
            rows = slice(h * 64, (h + 1) * 64)
            both = jnp.concatenate([out[rows].reshape(8, 8, 128), grads[rows].reshape(8, 8, 128)], axis=1)
            pp[:, :, (t * 4 + h) * 128 : (t * 4 + h + 1) * 128] = both.astype(bf16)
    back += give_back(1, pp, pp_out.at[:, columns(g, 1024)], OTHER + OWN)
    cand_final(dkc, ck_in, kcand_moves, ck_sum)
    back += give_back(4, ck_sum, ck_out.at[:, columns(g, 128)], OTHER + OWN)
    ksum = final(zk, zk_in, k_hops)
    both = jnp.concatenate([ksum.reshape(8, 8, 128), vsum[...].reshape(8, 8, 128)], axis=1)
    psum[...] = both.astype(bf16)
    back += give_back(5, psum, kvp_out.at[:, columns(g, 128)], OTHER + OWN)
    wait(back)


def finish_kernel(oc, dqc, pp, kvp, ck, cv, prompt_out, prompt_dq, prompt_dk, prompt_dv, oc_out, dqc_out, ck_out, cv_out, sems):
    copies = [
        pltpu.make_async_copy(source, target, sems.at[i])
        for i, (source, target) in enumerate(((oc, oc_out), (dqc, dqc_out), (ck, ck_out), (cv, cv_out)))
    ]
    start(copies)
    for source, upper, lower in ((pp, prompt_out, prompt_dq), (kvp, prompt_dk, prompt_dv)):
        both = source[...].astype(f32)
        upper[...] = both[0:8].astype(bf16)
        lower[...] = both[8:16].astype(bf16)
    wait(copies)


ANY = pl.BlockSpec(memory_space=pl.ANY)
VMEM = pl.BlockSpec(memory_space=pltpu.VMEM)
SMEM = pl.BlockSpec(memory_space=pltpu.SMEM)


def local(
    prompt_q, prompt_k, prompt_v, prompt_dout, cand_q, cand_k, cand_v, cand_dout, cand_len, placement
):
    DMA = pltpu.SemaphoreType.DMA

    def half(*shape):
        return pltpu.VMEM(shape, bf16)

    def full(*shape):
        return pltpu.VMEM(shape, f32)

    def result(*shape):
        return jax.ShapeDtypeStruct(shape, bf16)

    oc, dqc, pp, kvp, ck, cv = pl.pallas_call(
        kernel,
        out_shape=(
            result(32, 8192), result(32, 8192), result(16, 8192), result(16, 1024), result(32, 1024), result(32, 1024)
        ),
        in_specs=[SMEM] * 2 + [VMEM] * 4 + [ANY] * 4,
        out_specs=(ANY,) * 6,
        scratch_shapes=[
            half(16, 8192), half(16, 1024), half(8, 16, 128), half(4, 8, 32, 128), half(4, 8, 32, 128),
            half(8, 32, 1024), half(8, 16, 1024), half(8, 32, 1024), half(4, 8, 64, 128), half(4, 8, 64, 128),
            half(LANES, 128), half(LANES, 128), half(2, SPAN, 128), half(2, SPAN, 128),
            half(128, PROMPT), half(128, PROMPT), half(2, 128, SPAN), half(2, 128, SPAN),
            full(KEYS, LANES), half(KEYS, LANES), full(8, LANES), full(8, LANES), full(8, LANES), full(512, 128), full(128, LANES),
            half(8, 32, 1024), half(8, 32, 1024), half(8, 16, 1024),
            half(3, 8, 64, 128), half(3, 8, 64, 128), half(3, 8, 64, 128), half(3, 8, 64, 128),
            half(8, 64, 128), half(8, 64, 128), half(7, 64, 128), half(7, 64, 128),
            full(8, 64, 128), full(8, 64, 128), full(64, 128),
            half(4, 8, 32, 128), half(4, 8, 32, 128), half(3, 8, 32, 128), half(3, 8, 32, 128),
            half(8, 32, 128), half(8, 32, 128), half(8, 16, 128),
            DMA((12,)), DMA((6, 8)), DMA((6, 8)), DMA((4, 8)), DMA((4, 8)), DMA((4, 4, 8)), DMA((4, 4, 8)),
            DMA((14,)), DMA((14,)), DMA((6, 8)), DMA((6, 8)),
        ],
        compiler_params=pltpu.CompilerParams(
            collective_id=0, has_side_effects=True, vmem_limit_bytes=56 * 2**20
        ),
        name="layer",
    )(
        cand_len, placement,
        prompt_q, prompt_k, prompt_v, prompt_dout, cand_q, cand_k, cand_v, cand_dout,
    )
    return pl.pallas_call(
        finish_kernel,
        out_shape=(
            result(8, 8192), result(8, 8192), result(8, 1024), result(8, 1024),
            result(32, 8192), result(32, 8192), result(32, 1024), result(32, 1024),
        ),
        in_specs=[ANY, ANY, VMEM, VMEM, ANY, ANY],
        out_specs=(VMEM,) * 4 + (ANY,) * 4,
        scratch_shapes=[DMA((4,))],
        name="finish",
    )(oc, dqc, pp, kvp, ck, cv)


def solution(mesh):
    rows = P(("seq", "head"), None)
    return jax.shard_map(
        local,
        mesh=mesh,
        in_specs=(rows,) * 8 + (P(), P()),
        out_specs=(rows,) * 8,
        check_vma=False,
    )
```

```python
import functools
import math

import jax
import jax.numpy as jnp
from jax import lax
from jax.experimental import pallas as pl
from jax.experimental.pallas import tpu as pltpu
from jax.sharding import PartitionSpec as P

HD = 128
SCALE = 1.0 / math.sqrt(HD)
SCALE2 = SCALE * math.log2(math.e)
MESH = pl.DeviceIdType.MESH
f32, bf16 = jnp.float32, jnp.bfloat16
HIDDEN = -1e30
PART = 512
PROMPT, SPAN = 2048, 512
KEYS = PROMPT + SPAN
LANES = 2560
WIDE = 512


def coords():
    seq, head = lax.axis_index("seq"), lax.axis_index("head")
    x, y = seq % 4, (seq // 4) % 4
    z = (head // 2) * 2 + seq // 16
    return x, y, z, head % 2


def device(x, y, z, core):
    return ((z % 2) * 16 + y * 4 + x, (z // 2) * 2 + core)


def roles(x, y, core):
    xg, sx, yg, sy = x // 2, x % 2, y // 2, y % 2
    j = sy * 4 + sx * 2 + core
    g = ((sy + yg) % 2) * 4 + ((sx + xg) % 2) * 2 + core
    return xg, yg, j, g


def flip(value, bits):
    out = 0
    for bit in (4, 2, 1):
        digit = (value // bit) % 2
        out = out + bit * ((1 - digit) if bits & bit else digit)
    return out


def block_partner(x, y, z, core, d):
    px = x // 2 * 2 + (1 - x % 2 if d & 2 else x % 2)
    py = y // 2 * 2 + (1 - y % 2 if d & 4 else y % 2)
    return device(px, py, z, 1 - core if d & 1 else core)


def greet(partners):
    barrier = pltpu.get_barrier_semaphore()
    for partner in partners:
        pl.semaphore_signal(barrier, inc=1, device_id=partner, device_id_type=MESH)
    pl.semaphore_wait(barrier, len(partners))


def remote(src, dst, send, recv, target):
    return pltpu.make_async_remote_copy(
        src_ref=src, dst_ref=dst, send_sem=send, recv_sem=recv, device_id=target, device_id_type=MESH
    )


def start(copies):
    for copy in copies:
        copy.start()


def take(sem, ref):
    pltpu.make_async_copy(ref, ref, sem).wait()


def nt(a, b):
    return lax.dot_general(a, b, (((1,), (1,)), ((), ())), preferred_element_type=f32)


def nn(a, b):
    return lax.dot_general(a, b, (((1,), (0,)), ((), ())), preferred_element_type=f32)


def columns(index, width):
    return pl.ds(pl.multiple_of(index * width, width), width)


def kernel(
    cand_len_in, placement_in,
    prompt_q, prompt_k, prompt_v, prompt_dout, cand_q, cand_k, cand_v, cand_dout,
    oc_out, dqc_out, pp_out, kvp_out, ck_out, cv_out,
    pp_stage, kv_stage, kvp_in, kc, vc, qc_in, pp_in, gc_in, kq, vq,
    q_all, g_all, ks, vs, kpt, vpt, kst, vst,
    scores, halves, peaks, shares, deltas, prompt_out, dq,
    oc, dqc, pp, dvb, dkb, rv, rk, zv, zk, zv_in, zk_in, dvown, dkown, vsum,
    dvc, dkc, cv_in, ck_in, cv_sum, ck_sum, psum,
    cand_len, placement, lsem, asend, arecv, zsend, zrecv, msend, mrecv, csend, crecv, bsend, brecv,
):
    x, y, z, core = coords()
    xg, yg, j, g = roles(x, y, core)
    zhi, sy = z // 2, y % 2
    block = {d: block_partner(x, y, z, core, d) for d in range(1, 8)}
    mirror = {
        1: device(3 - x, y, z, core), 2: device(x, 3 - y, z, core), 3: device(3 - x, 3 - y, z, core)
    }
    column = {d: device(x, y, (z + d) % 8, core) for d in range(1, 8)}

    small = [
        pltpu.make_async_copy(cand_len_in, cand_len, lsem.at[0]),
        pltpu.make_async_copy(placement_in, placement, lsem.at[1]),
    ]
    start(small)
    both = jnp.concatenate([prompt_k[...].astype(f32), prompt_v[...].astype(f32)], axis=0)
    kv_stage[...] = both.astype(bf16)
    both = jnp.concatenate([prompt_q[...].astype(f32), prompt_dout[...].astype(f32)], axis=0)
    pp_stage[...] = both.astype(bf16)

    greet(list(block.values()) + list(mirror.values()) + list(column.values()))

    late = []

    def exchange(kind, source, width, target):
        start([pltpu.make_async_copy(source.at[:, columns(g, width)], target.at[j], arecv.at[kind])])
        start(
            [
                remote(source.at[:, columns(flip(g, d), width)], target.at[j], asend.at[kind], arecv.at[kind], block[d])
                for d in range(1, 8)
            ]
        )
        late.append((asend.at[kind], target.at[pl.ds(0, 7)]))

    exchange(0, kv_stage, 128, kvp_in)
    exchange(1, cand_k, 128, kc.at[zhi])
    exchange(2, cand_q, 1024, qc_in)
    exchange(3, pp_stage, 1024, pp_in)
    exchange(4, cand_v, 128, vc.at[zhi])
    exchange(5, cand_dout, 1024, gc_in)

    below, above = (zhi + 3) % 4, (zhi + 1) % 4
    first, second = pl.ds(0, 4), pl.ds(4, 4)

    def along_z_in(which, kind):
        start(
            [
                remote(which.at[0, z], which.at[0, z], zsend.at[kind], zrecv.at[kind], column[d])
                for d in (1, 7, 2, 6, 3, 5, 4)
            ]
        )
        late.append((zsend.at[kind], which.at[0, pl.ds(0, 7)]))

    def quadrants(which, kind):
        take(zrecv.at[kind], which.at[0, pl.ds(0, 7)])
        start(
            [
                remote(which.at[0], which.at[p], msend.at[kind], mrecv.at[kind, p], mirror[p])
                for p in (1, 2, 3)
            ]
        )
        late.append((msend.at[kind], which.at[pl.ds(0, 3)]))

    def near(which, kind):
        take(arecv.at[1 + 3 * kind], which.at[zhi])
        start(
            [
                remote(which.at[zhi], which.at[zhi], csend.at[kind], crecv.at[kind], column[d])
                for d in (2, 6)
            ]
        )
        late.append((csend.at[kind], which.at[pl.ds(0, 2)]))

    def far(which, kind):
        take(crecv.at[kind], which.at[pl.ds(0, 2)])
        start(
            [
                remote(which.at[below, first], which.at[below, first], csend.at[2 + kind], crecv.at[2 + kind], column[2]),
                remote(which.at[above, second], which.at[above, second], csend.at[2 + kind], crecv.at[2 + kind], column[6]),
            ]
        )
        late.append((csend.at[2 + kind], which.at[0]))

    take(arecv.at[0], kvp_in)
    both = kvp_in[...].astype(f32)
    kq[0, z] = both[:, 0:8, :].reshape(64, 128).astype(bf16)
    vq[0, z] = both[:, 8:16, :].reshape(64, 128).astype(bf16)
    along_z_in(kq, 0)
    near(kc, 0)
    along_z_in(vq, 1)
    quadrants(kq, 0)
    far(kc, 0)
    near(vc, 1)
    quadrants(vq, 1)

    slots = (1 - sy, sy)
    take(arecv.at[2], qc_in)
    for i in range(2):
        for k in range(4):
            rows = qc_in[slots[i] * 4 + k]
            for h in range(8):
                at = i * 1024 + h * 128 + k * 32
                q_all[at : at + 32, :] = rows[:, h * 128 : (h + 1) * 128]
    take(arecv.at[3], pp_in)
    for h in range(8):
        both = pp_in[:, :, h * 128 : (h + 1) * 128].astype(f32)
        at = 2048 + h * 64
        q_all[at : at + 64, :] = both[:, 0:8, :].reshape(64, 128).astype(bf16)
        g_all[at : at + 64, :] = both[:, 8:16, :].reshape(64, 128).astype(bf16)

    peaks[...] = jnp.full(peaks.shape, HIDDEN, f32)
    lane = lax.broadcasted_iota(jnp.int32, (1, WIDE), 1)
    cand_at = ((lane // 64) % 2) * 256 + zhi * 64 + lane % 64
    prompt_at = (
        (z % 2) * 1024 + zhi * 16 + yg * 512 + xg * 128
        + ((lane // 32) % 2) * 256 + ((lane // 16) % 2) * 64 + ((lane // 8) % 2) * 8 + lane % 8
    )

    def top(s):
        return jnp.max(s.reshape(-1, 8, WIDE), axis=0)

    def score_part(p):
        rows = slice(p * PART, (p + 1) * PART)
        keys = kq[p].reshape(PART, 128)

        def cand(t, carry):
            at = columns(t, WIDE)
            s = nt(keys, q_all[at, :])
            scores[rows, at] = s
            peaks[:, at] = jnp.maximum(peaks[:, at], top(s))
            return carry

        lax.fori_loop(0, 4, cand, 0, unroll=2)
        n = lax.broadcasted_iota(jnp.int32, (PART, 1), 0)
        zz = n // 64
        ygp = yg if p < 2 else 1 - yg
        xgp = xg if p % 2 == 0 else 1 - xg
        key_at = (
            (zz % 2) * 1024 + (zz // 2) * 16 + ygp * 512 + ((n // 32) % 2) * 256
            + xgp * 128 + ((n // 16) % 2) * 64 + ((n // 8) % 2) * 8 + n % 8
        )

        s = jnp.where(key_at <= prompt_at, nt(keys, q_all[2048:, :]), HIDDEN)
        scores[rows, 2048:] = s
        peaks[:, 2048:] = jnp.maximum(peaks[:, 2048:], top(s))
        kpt[:, rows] = keys.astype(f32).T.astype(bf16)

    score_part(0)
    for p in (1, 2, 3):
        take(mrecv.at[0, p], kq.at[p])
        score_part(p)

    def slot_rows(source, target, turned):
        for i in range(2):
            for half in range(2):
                for hi in range(4):
                    for c in range(2):
                        at = half * 256 + hi * 64 + c * 32
                        target[i, at : at + 32, :] = source[hi, slots[i] * 4 + half * 2 + c]
            turned[i] = target[i].astype(f32).T.astype(bf16)

    far(vc, 1)
    take(crecv.at[2], kc.at[0])
    slot_rows(kc, ks, kst)
    span_at = lax.broadcasted_iota(jnp.int32, (SPAN, 1), 0)

    def score_slot(t, carry):
        at = columns(t, WIDE)
        s = jnp.where(span_at <= cand_at, nt(ks[t // 2], q_all[at, :]), HIDDEN)
        scores[PROMPT:, at] = s
        peaks[:, at] = jnp.maximum(peaks[:, at], top(s))
        return carry

    lax.fori_loop(0, 4, score_slot, 0, unroll=2)

    small[0].wait()
    small[1].wait()
    lengths = []
    for i in range(2):
        slot = (z % 2) * 8 + ((y // 2) * 2 + slots[i]) * 2 + x // 2
        length = jnp.int32(0)
        for c in range(16):
            length = length + jnp.where(placement[c] == slot, cand_len[c], 0)
        lengths.append(length)
    take(arecv.at[5], gc_in)
    row = lax.broadcasted_iota(jnp.int32, (32, 1), 0)
    for i in range(2):
        for k in range(4):
            kept = (k // 2) * 256 + zhi * 64 + (k % 2) * 32 + row < lengths[i]
            rows = jnp.where(kept, gc_in[slots[i] * 4 + k].astype(f32), 0.0).astype(bf16)
            for h in range(8):
                at = i * 1024 + h * 128 + k * 32
                g_all[at : at + 32, :] = rows[:, h * 128 : (h + 1) * 128]
    for p in (1, 2, 3):
        take(mrecv.at[1, p], vq.at[p])
    for p in range(4):
        vpt[:, p * PART : (p + 1) * PART] = vq[p].reshape(PART, 128).astype(f32).T.astype(bf16)
    take(crecv.at[3], vc.at[0])
    slot_rows(vc, vs, vst)

    def weigh(t, cand, i):
        at = columns(t, 256)
        parts = KEYS // PART if cand else PROMPT // PART
        peak = jnp.max(peaks[:, at], axis=0, keepdims=True)
        total = jnp.zeros((8, 256), f32)
        for p in range(parts):
            rows = slice(p * PART, (p + 1) * PART)
            e = jnp.exp2((scores[rows, at] - peak) * SCALE2)
            scores[rows, at] = e
            total = total + jnp.sum(e.reshape(-1, 8, 256), axis=0)
        share = 1.0 / jnp.sum(total, axis=0, keepdims=True)
        shares[:, at] = jnp.broadcast_to(share, (8, 256))
        for p in range(parts):
            rows = slice(p * PART, (p + 1) * PART)
            halves[rows, at] = (scores[rows, at] * share).astype(bf16)
        out = nn(vpt[...], halves[0:PROMPT, at])
        if cand:
            out = out + nn(vst[i], halves[PROMPT:, at])
            out = jnp.where(cand_at[:, 0:256] < lengths[i], out, 0.0)
        delta = jnp.sum(out * g_all[at, :].astype(f32).T, axis=0, keepdims=True)
        deltas[:, at] = jnp.broadcast_to(delta, (8, 256))
        return out.T

    def put_cand(target, i, pair, rows):
        for a in range(2):
            for k in range(4):
                at = a * 128 + k * 32
                target[slots[i] * 4 + k, :, columns(pair * 2 + a, 128)] = rows[at : at + 32, :].astype(bf16)

    def give_back(kind, source, target, width, which):
        here = target.at[:, columns(g, width)]
        if 0 in which:
            start([pltpu.make_async_copy(source.at[j], here, brecv.at[kind])])
            late.append((bsend.at[kind], source.at[pl.ds(0, 7)]))
            late.append((brecv.at[kind], target))
        start([remote(source.at[flip(j, d)], here, bsend.at[kind], brecv.at[kind], block[d]) for d in which if d])

    OTHER, OWN = (4, 5, 6, 7), (1, 2, 3, 0)
    for i, which in enumerate((OTHER, OWN)):

        def weigh_cand(pair, carry, i=i):
            put_cand(oc, i, pair, weigh(i * 4 + pair, True, i))
            return carry

        lax.fori_loop(0, 4, weigh_cand, 0, unroll=2)
        give_back(0, oc, oc_out, 1024, which)

    def weigh_prompt(t, carry):
        prompt_out[columns(t, 256), :] = weigh(8 + t, False, None)
        return carry

    lax.fori_loop(0, 2, weigh_prompt, 0, unroll=2)

    def cand_terms(sums, target, i):
        for half in range(2):
            for hi in range(4):
                for c in range(2):
                    at = half * 256 + hi * 64 + c * 32
                    target[hi, slots[i] * 4 + half * 2 + c] = sums[at : at + 32, :].astype(bf16)

    def slot_terms(others, scale, box, inbox, kind):
        for i in range(2):
            rows = slice(i * 1024, (i + 1) * 1024)
            cand_terms(nn(halves[PROMPT:, rows], others[rows, :]) * scale, box, i)
        start(
            [
                remote(box.at[(zhi + n) % 4], inbox.at[n - 1], csend.at[4 + kind], crecv.at[4 + kind], column[2 * n])
                for n in (1, 2, 3)
            ]
        )
        late.append((csend.at[4 + kind], inbox))

    def terms(others, scale, boxes, mine, inbox, kind, p):
        total = nn(halves[p * PART : (p + 1) * PART, :], others[...]) * scale
        if p == 0:
            mine[...] = total.reshape(8, 64, 128)
            late.append((msend.at[2 + kind], inbox))
            return
        boxes[p - 1] = total.reshape(8, 64, 128).astype(bf16)
        start([remote(boxes.at[p - 1], inbox.at[p - 1], msend.at[2 + kind], mrecv.at[2 + kind, 0], mirror[p])])

    def along_z(mine, inbox, stage, landed, kind):
        take(mrecv.at[2 + kind, 0], inbox)
        total = mine[...] + inbox[0].astype(f32) + inbox[1].astype(f32) + inbox[2].astype(f32)
        stage[...] = total.astype(bf16)
        start(
            [
                remote(stage.at[(z + d) % 8], landed.at[d - 1], zsend.at[2 + kind], zrecv.at[2 + kind], column[d])
                for d in (4, 3, 5, 2, 6, 1, 7)
            ]
        )
        late.append((zsend.at[2 + kind], landed))

    def final(stage, landed, kind):
        take(zrecv.at[2 + kind], landed)
        total = stage[z].astype(f32)
        for d in range(7):
            total = total + landed[d].astype(f32)
        return total

    def cand_final(box, inbox, total, kind):
        take(crecv.at[4 + kind], inbox)
        total[...] = (
            box[zhi].astype(f32) + inbox[0].astype(f32) + inbox[1].astype(f32) + inbox[2].astype(f32)
        ).astype(bf16)

    FARTHEST = (3, 1, 2, 0)
    slot_terms(g_all, 1.0, dvc, cv_in, 0)
    for p in FARTHEST:
        terms(g_all, 1.0, dvb, dvown, rv, 0, p)

    def grade(values, turned, rows, at):
        dw = nt(values, g_all[at, :])
        ds = (scores[rows, at] * shares[0:1, at] * (dw - deltas[0:1, at])).astype(bf16)
        halves[rows, at] = ds
        return nn(turned, ds)

    def grade_slot(t, carry):
        at = columns(t, WIDE)
        dq[:, at] = grade(vs[t // 2], kst[t // 2], slice(PROMPT, KEYS), at)
        return carry

    lax.fori_loop(0, 4, grade_slot, 0, unroll=2)
    dq[:, 2048:] = jnp.zeros((128, WIDE), f32)
    slot_terms(q_all, SCALE, dkc, ck_in, 1)

    def grade_part(p, first, last):
        rows = slice(p * PART, (p + 1) * PART)

        def body(t, carry):
            at = columns(t, WIDE)
            dq[:, at] += grade(vq[p].reshape(PART, 128), kpt[:, rows], rows, at)
            return carry

        lax.fori_loop(first, last, body, 0, unroll=2)

    for n, p in enumerate(FARTHEST[:3]):
        grade_part(p, 0, 5)
        terms(q_all, SCALE, dkb, dkown, rk, 1, p)
        if n == 0:
            along_z(dvown, rv, zv, zv_in, 0)
            cand_final(dvc, cv_in, cv_sum, 0)
            give_back(3, cv_sum, cv_out, 128, OTHER + OWN)
    vsum[...] = final(zv, zv_in, 0)
    for i, which in enumerate((OTHER, OWN)):
        grade_part(0, i * 2, i * 2 + 2)
        for pair in range(4):
            t = i * 4 + pair
            put_cand(dqc, i, pair, (dq[:, t * 256 : (t + 1) * 256] * SCALE).T)
        give_back(2, dqc, dqc_out, 1024, which)
    grade_part(0, 4, 5)
    terms(q_all, SCALE, dkb, dkown, rk, 1, 0)
    along_z(dkown, rk, zk, zk_in, 1)
    for t in range(2):
        out = prompt_out[t * 256 : (t + 1) * 256, :]
        grads = (dq[:, 2048 + t * 256 : 2304 + t * 256] * SCALE).T
        for h in range(4):
            rows = slice(h * 64, (h + 1) * 64)
            both = jnp.concatenate([out[rows].reshape(8, 8, 128), grads[rows].reshape(8, 8, 128)], axis=1)
            pp[:, :, (t * 4 + h) * 128 : (t * 4 + h + 1) * 128] = both.astype(bf16)
    give_back(1, pp, pp_out, 1024, OTHER + OWN)
    cand_final(dkc, ck_in, ck_sum, 1)
    give_back(4, ck_sum, ck_out, 128, OTHER + OWN)
    ksum = final(zk, zk_in, 1)
    both = jnp.concatenate([ksum.reshape(8, 8, 128), vsum[...].reshape(8, 8, 128)], axis=1)
    psum[...] = both.astype(bf16)
    give_back(5, psum, kvp_out, 128, OTHER + OWN)
    for sem, ref in late:
        take(sem, ref)


def finish_kernel(oc, dqc, pp, kvp, ck, cv, prompt_out, prompt_dq, prompt_dk, prompt_dv, oc_out, dqc_out, ck_out, cv_out, sems):
    copies = [
        pltpu.make_async_copy(source, target, sems.at[i])
        for i, (source, target) in enumerate(((oc, oc_out), (dqc, dqc_out), (ck, ck_out), (cv, cv_out)))
    ]
    start(copies)
    for source, upper, lower in ((pp, prompt_out, prompt_dq), (kvp, prompt_dk, prompt_dv)):
        both = source[...].astype(f32)
        upper[...] = both[0:8].astype(bf16)
        lower[...] = both[8:16].astype(bf16)
    for copy in copies:
        copy.wait()


ANY = pl.BlockSpec(memory_space=pl.ANY)
VMEM = pl.BlockSpec(memory_space=pltpu.VMEM)


def local(
    prompt_q, prompt_k, prompt_v, prompt_dout, cand_q, cand_k, cand_v, cand_dout, cand_len, placement
):
    DMA = pltpu.SemaphoreType.DMA

    def half(*shape):
        return pltpu.VMEM(shape, bf16)

    def full(*shape):
        return pltpu.VMEM(shape, f32)

    def result(*shape):
        return jax.ShapeDtypeStruct(shape, bf16)

    oc, dqc, pp, kvp, ck, cv = pl.pallas_call(
        kernel,
        out_shape=(
            result(32, 8192), result(32, 8192), result(16, 8192), result(16, 1024), result(32, 1024), result(32, 1024)
        ),
        in_specs=[ANY] * 2 + [VMEM] * 4 + [ANY] * 4,
        out_specs=(ANY,) * 6,
        scratch_shapes=[
            half(16, 8192), half(16, 1024), half(8, 16, 128), half(4, 8, 32, 128), half(4, 8, 32, 128),
            half(8, 32, 1024), half(8, 16, 1024), half(8, 32, 1024), half(4, 8, 64, 128), half(4, 8, 64, 128),
            half(LANES, 128), half(LANES, 128), half(2, SPAN, 128), half(2, SPAN, 128),
            half(128, PROMPT), half(128, PROMPT), half(2, 128, SPAN), half(2, 128, SPAN),
            full(KEYS, LANES), half(KEYS, LANES), full(8, LANES), full(8, LANES), full(8, LANES), full(512, 128), full(128, LANES),
            half(8, 32, 1024), half(8, 32, 1024), half(8, 16, 1024),
            half(3, 8, 64, 128), half(3, 8, 64, 128), half(3, 8, 64, 128), half(3, 8, 64, 128),
            half(8, 64, 128), half(8, 64, 128), half(7, 64, 128), half(7, 64, 128),
            full(8, 64, 128), full(8, 64, 128), full(64, 128),
            half(4, 8, 32, 128), half(4, 8, 32, 128), half(3, 8, 32, 128), half(3, 8, 32, 128),
            half(8, 32, 128), half(8, 32, 128), half(8, 16, 128),
            pltpu.SMEM((16,), jnp.int32), pltpu.SMEM((16,), jnp.int32),
            DMA((2,)), DMA((6,)), DMA((6,)), DMA((4,)), DMA((4,)), DMA((4,)), DMA((4, 4)),
            DMA((6,)), DMA((6,)), DMA((6,)), DMA((6,)),
        ],
        compiler_params=pltpu.CompilerParams(
            collective_id=0, has_side_effects=True, vmem_limit_bytes=56 * 2**20
        ),
        name="layer",
    )(
        cand_len, placement,
        prompt_q, prompt_k, prompt_v, prompt_dout, cand_q, cand_k, cand_v, cand_dout,
    )
    return pl.pallas_call(
        finish_kernel,
        out_shape=(
            result(8, 8192), result(8, 8192), result(8, 1024), result(8, 1024),
            result(32, 8192), result(32, 8192), result(32, 1024), result(32, 1024),
        ),
        in_specs=[VMEM] * 6,
        out_specs=(VMEM,) * 4 + (ANY,) * 4,
        scratch_shapes=[DMA((4,))],
        name="finish",
    )(oc, dqc, pp, kvp, ck, cv)


def solution(mesh):
    rows = P(("seq", "head"), None)
    return jax.shard_map(
        local,
        mesh=mesh,
        in_specs=(rows,) * 8 + (P(), P()),
        out_specs=(rows,) * 8,
        check_vma=False,
    )
```

```python
import functools
import math

import jax
import jax.numpy as jnp
from jax import lax
from jax.experimental import pallas as pl
from jax.experimental.pallas import tpu as pltpu
from jax.sharding import PartitionSpec as P

HD = 128
SCALE = 1.0 / math.sqrt(HD)
SCALE2 = SCALE * math.log2(math.e)
MESH = pl.DeviceIdType.MESH
f32, bf16 = jnp.float32, jnp.bfloat16
HIDDEN = -1e30
PART = 512
PROMPT, SPAN = 2048, 512
KEYS = PROMPT + SPAN
LANES = 2560
WIDE = 512


def coords():
    seq, head = lax.axis_index("seq"), lax.axis_index("head")
    x, y = seq % 4, (seq // 4) % 4
    z = (head // 2) * 2 + seq // 16
    return x, y, z, head % 2


def device(x, y, z, core):
    return ((z % 2) * 16 + y * 4 + x, (z // 2) * 2 + core)


def roles(x, y, core):
    xg, sx, yg, sy = x // 2, x % 2, y // 2, y % 2
    j = sy * 4 + sx * 2 + core
    g = ((sy + yg) % 2) * 4 + ((sx + xg) % 2) * 2 + core
    return xg, yg, j, g


def flip(value, bits):
    out = 0
    for bit in (4, 2, 1):
        digit = (value // bit) % 2
        out = out + bit * ((1 - digit) if bits & bit else digit)
    return out


def block_partner(x, y, z, core, d):
    px = x // 2 * 2 + (1 - x % 2 if d & 2 else x % 2)
    py = y // 2 * 2 + (1 - y % 2 if d & 4 else y % 2)
    return device(px, py, z, 1 - core if d & 1 else core)


def greet(partners):
    barrier = pltpu.get_barrier_semaphore()
    for partner in partners:
        pl.semaphore_signal(barrier, inc=1, device_id=partner, device_id_type=MESH)
    pl.semaphore_wait(barrier, len(partners))


def remote(src, dst, send, recv, target):
    return pltpu.make_async_remote_copy(
        src_ref=src, dst_ref=dst, send_sem=send, recv_sem=recv, device_id=target, device_id_type=MESH
    )


def start(copies):
    for copy in copies:
        copy.start()


def take(sem, ref):
    pltpu.make_async_copy(ref, ref, sem).wait()


def nt(a, b):
    return lax.dot_general(a, b, (((1,), (1,)), ((), ())), preferred_element_type=f32)


def nn(a, b):
    return lax.dot_general(a, b, (((1,), (0,)), ((), ())), preferred_element_type=f32)


def columns(index, width):
    if isinstance(index, int):
        return pl.ds(index * width, width)
    return pl.ds(pl.multiple_of(index * width, width), width)


def kernel(
    cand_len_in, placement_in,
    prompt_q, prompt_k, prompt_v, prompt_dout, cand_q, cand_k, cand_v, cand_dout,
    oc_out, dqc_out, pp_out, kvp_out, ck_out, cv_out,
    pp_stage, kv_stage, kvp_in, kc, vc, qc_in, pp_in, gc_in, kq, vq,
    q_all, g_all, ks, vs, kpt, vpt, kst, vst,
    scores, halves, slot_scores, slot_halves, peaks, shares, deltas, prompt_out, dq,
    dvb, dkb, rv, rk, zv, zk, zv_in, zk_in, dvown, dkown, vsum,
    dvc, dkc, cv_in, ck_in, cv_sum, ck_sum, psum,
    cand_len, placement, lsem, asend, arecv, zsend, zrecv, msend, mrecv, csend, crecv, bsend, brecv,
):
    x, y, z, core = coords()
    xg, yg, j, g = roles(x, y, core)
    zhi, sy = z // 2, y % 2
    block = {d: block_partner(x, y, z, core, d) for d in range(1, 8)}
    mirror = {
        1: device(3 - x, y, z, core), 2: device(x, 3 - y, z, core), 3: device(3 - x, 3 - y, z, core)
    }
    column = {d: device(x, y, (z + d) % 8, core) for d in range(1, 8)}

    small = [
        pltpu.make_async_copy(cand_len_in, cand_len, lsem.at[0]),
        pltpu.make_async_copy(placement_in, placement, lsem.at[1]),
    ]
    start(small)
    both = jnp.concatenate([prompt_k[...].astype(f32), prompt_v[...].astype(f32)], axis=0)
    kv_stage[...] = both.astype(bf16)
    both = jnp.concatenate([prompt_q[...].astype(f32), prompt_dout[...].astype(f32)], axis=0)
    pp_stage[...] = both.astype(bf16)

    greet(list(block.values()) + list(mirror.values()) + list(column.values()))

    late = []

    def exchange(kind, source, width, target):
        start([pltpu.make_async_copy(source.at[:, columns(g, width)], target.at[j], arecv.at[kind])])
        start(
            [
                remote(source.at[:, columns(flip(g, d), width)], target.at[j], asend.at[kind], arecv.at[kind], block[d])
                for d in range(1, 8)
            ]
        )
        late.append((asend.at[kind], target.at[pl.ds(0, 7)]))

    exchange(0, kv_stage, 128, kvp_in)
    exchange(1, cand_k, 128, kc.at[zhi])
    exchange(2, cand_q, 1024, qc_in)
    exchange(3, pp_stage, 1024, pp_in)
    exchange(4, cand_v, 128, vc.at[zhi])
    exchange(5, cand_dout, 1024, gc_in)

    CLOSE, DISTANT = (1, 7, 2, 6), (3, 5, 4)
    below, above = (zhi + 3) % 4, (zhi + 1) % 4
    first, second = pl.ds(0, 4), pl.ds(4, 4)

    def along_z_in(which, kind):
        start(
            [
                remote(
                    which.at[0, z], which.at[0, z], zsend.at[kind],
                    zrecv.at[kind if d in CLOSE else 4 + kind], column[d],
                )
                for d in CLOSE + DISTANT
            ]
        )
        late.append((zsend.at[kind], which.at[0, pl.ds(0, 7)]))

    def forward(which, kind, steps):
        for d in steps:
            at = (z + 8 - d) % 8
            start([remote(which.at[0, at], which.at[p, at], msend.at[kind], mrecv.at[kind, p], mirror[p]) for p in (1, 2, 3)])

    def quadrants(which, kind):
        forward(which, kind, (0,))
        take(zrecv.at[kind], which.at[0, pl.ds(0, 4)])
        forward(which, kind, CLOSE)
        take(zrecv.at[4 + kind], which.at[0, pl.ds(0, 3)])
        forward(which, kind, DISTANT)
        late.append((msend.at[kind], which.at[pl.ds(0, 3)]))

    def near(which, kind):
        take(arecv.at[1 + 3 * kind], which.at[zhi])
        start(
            [
                remote(which.at[zhi], which.at[zhi], csend.at[kind], crecv.at[kind], column[d])
                for d in (2, 6)
            ]
        )
        late.append((csend.at[kind], which.at[pl.ds(0, 2)]))

    def far(which, kind):
        take(crecv.at[kind], which.at[pl.ds(0, 2)])
        start(
            [
                remote(which.at[below, first], which.at[below, first], csend.at[2 + kind], crecv.at[2 + kind], column[2]),
                remote(which.at[above, second], which.at[above, second], csend.at[2 + kind], crecv.at[2 + kind], column[6]),
            ]
        )
        late.append((csend.at[2 + kind], which.at[0]))

    take(arecv.at[0], kvp_in)
    both = kvp_in[...].astype(f32)
    kq[0, z] = both[:, 0:8, :].reshape(64, 128).astype(bf16)
    vq[0, z] = both[:, 8:16, :].reshape(64, 128).astype(bf16)
    along_z_in(kq, 0)
    near(kc, 0)
    along_z_in(vq, 1)
    quadrants(kq, 0)
    far(kc, 0)
    near(vc, 1)
    quadrants(vq, 1)

    slots = (1 - sy, sy)
    take(arecv.at[2], qc_in)
    for i in range(2):
        for k in range(4):
            rows = qc_in[slots[i] * 4 + k]
            for h in range(8):
                at = i * 1024 + h * 128 + k * 32
                q_all[at : at + 32, :] = rows[:, h * 128 : (h + 1) * 128]
    take(arecv.at[3], pp_in)
    for h in range(8):
        both = pp_in[:, :, h * 128 : (h + 1) * 128].astype(f32)
        at = 2048 + h * 64
        q_all[at : at + 64, :] = both[:, 0:8, :].reshape(64, 128).astype(bf16)
        g_all[at : at + 64, :] = both[:, 8:16, :].reshape(64, 128).astype(bf16)

    lane = lax.broadcasted_iota(jnp.int32, (1, WIDE), 1)
    cand_at = ((lane // 64) % 2) * 256 + zhi * 64 + lane % 64
    prompt_at = (
        (z % 2) * 1024 + zhi * 16 + yg * 512 + xg * 128
        + ((lane // 32) % 2) * 256 + ((lane // 16) % 2) * 64 + ((lane // 8) % 2) * 8 + lane % 8
    )

    def part_scores(p):
        return slot_scores if p == 4 else scores.at[p * PART : (p + 1) * PART]

    def part_halves(p):
        return slot_halves if p == 4 else halves.at[p * PART : (p + 1) * PART]

    def weigh_part(p, at, s):
        peak = jnp.max(jnp.max(s.reshape(-1, 8, WIDE), axis=0), axis=0, keepdims=True)
        e = jnp.exp2((s - peak) * SCALE2)
        part_scores(p)[:, at] = e
        peaks[p, :, at] = jnp.broadcast_to(peak, (8, WIDE))
        shares[p, :, at] = jnp.sum(e.reshape(-1, 8, WIDE), axis=0)

    def score_part(p):
        rows = slice(p * PART, (p + 1) * PART)
        keys = kq[p].reshape(PART, 128)

        def cand(t, carry):
            at = columns(t, WIDE)
            weigh_part(p, at, nt(keys, q_all[at, :]))
            return carry

        lax.fori_loop(0, 4, cand, 0, unroll=4)
        n = lax.broadcasted_iota(jnp.int32, (PART, 1), 0)
        zz = n // 64
        ygp = yg if p < 2 else 1 - yg
        xgp = xg if p % 2 == 0 else 1 - xg
        key_at = (
            (zz % 2) * 1024 + (zz // 2) * 16 + ygp * 512 + ((n // 32) % 2) * 256
            + xgp * 128 + ((n // 16) % 2) * 64 + ((n // 8) % 2) * 8 + n % 8
        )

        weigh_part(p, pl.ds(2048, WIDE), jnp.where(key_at <= prompt_at, nt(keys, q_all[2048:, :]), HIDDEN))
        kpt[:, rows] = keys.astype(f32).T.astype(bf16)

    score_part(0)
    for p in (1, 2, 3):
        take(mrecv.at[0, p], kq.at[p])
        score_part(p)

    def slot_rows(source, target, turned):
        for i in range(2):
            for half in range(2):
                for hi in range(4):
                    for c in range(2):
                        at = half * 256 + hi * 64 + c * 32
                        target[i, at : at + 32, :] = source[hi, slots[i] * 4 + half * 2 + c]
            turned[i] = target[i].astype(f32).T.astype(bf16)

    far(vc, 1)
    take(crecv.at[2], kc.at[0])
    slot_rows(kc, ks, kst)
    span_at = lax.broadcasted_iota(jnp.int32, (SPAN, 1), 0)

    def score_slot(t, carry):
        at = columns(t, WIDE)
        weigh_part(4, at, jnp.where(span_at <= cand_at, nt(ks[t // 2], q_all[at, :]), HIDDEN))
        return carry

    lax.fori_loop(0, 4, score_slot, 0, unroll=2)

    def weigh(t, parts):
        at = columns(t, WIDE)
        tops = [peaks[p, 0:1, at] for p in range(parts)]
        peak = functools.reduce(jnp.maximum, tops)
        lifts = [jnp.exp2((top - peak) * SCALE2) for top in tops]
        sums = [jnp.sum(shares[p, :, at], axis=0, keepdims=True) for p in range(parts)]
        share = 1.0 / sum(lift * total for lift, total in zip(lifts, sums))
        for p in range(parts):
            lift = lifts[p] * share
            shares[p, :, at] = jnp.broadcast_to(lift, (8, WIDE))
            part_halves(p)[:, at] = (part_scores(p)[:, at] * lift).astype(bf16)

    for t in range(4):
        weigh(t, KEYS // PART)
    weigh(4, PROMPT // PART)

    small[0].wait()
    small[1].wait()
    lengths = []
    for i in range(2):
        slot = (z % 2) * 8 + ((y // 2) * 2 + slots[i]) * 2 + x // 2
        length = jnp.int32(0)
        for c in range(16):
            length = length + jnp.where(placement[c] == slot, cand_len[c], 0)
        lengths.append(length)
    take(arecv.at[5], gc_in)
    row = lax.broadcasted_iota(jnp.int32, (32, 1), 0)
    for i in range(2):
        for k in range(4):
            kept = (k // 2) * 256 + zhi * 64 + (k % 2) * 32 + row < lengths[i]
            rows = jnp.where(kept, gc_in[slots[i] * 4 + k].astype(f32), 0.0).astype(bf16)
            for h in range(8):
                at = i * 1024 + h * 128 + k * 32
                g_all[at : at + 32, :] = rows[:, h * 128 : (h + 1) * 128]
    def cand_terms(sums, target, i):
        for half in range(2):
            for hi in range(4):
                for c in range(2):
                    at = half * 256 + hi * 64 + c * 32
                    target[hi, slots[i] * 4 + half * 2 + c] = sums[at : at + 32, :].astype(bf16)

    def slot_terms(others, scale, box, inbox, kind):
        for i in range(2):
            rows = slice(i * 1024, (i + 1) * 1024)
            cand_terms(nn(slot_halves[:, rows], others[rows, :]) * scale, box, i)
        start(
            [
                remote(box.at[(zhi + n) % 4], inbox.at[n - 1], csend.at[4 + kind], crecv.at[4 + kind], column[2 * n])
                for n in (1, 2, 3)
            ]
        )
        late.append((csend.at[4 + kind], inbox))

    def terms(others, scale, boxes, mine, inbox, kind, p):
        total = nn(halves[p * PART : (p + 1) * PART, :], others[...]) * scale
        if p == 0:
            mine[...] = total.reshape(8, 64, 128)
            late.append((msend.at[2 + kind], inbox))
            return
        boxes[p - 1] = total.reshape(8, 64, 128).astype(bf16)
        start([remote(boxes.at[p - 1], inbox.at[p - 1], msend.at[2 + kind], mrecv.at[2 + kind, 0], mirror[p])])

    def along_z(mine, inbox, stage, landed, kind):
        take(mrecv.at[2 + kind, 0], inbox)
        total = mine[...] + inbox[0].astype(f32) + inbox[1].astype(f32) + inbox[2].astype(f32)
        stage[...] = total.astype(bf16)
        start(
            [
                remote(stage.at[(z + d) % 8], landed.at[d - 1], zsend.at[2 + kind], zrecv.at[2 + kind], column[d])
                for d in (4, 3, 5, 2, 6, 1, 7)
            ]
        )
        late.append((zsend.at[2 + kind], landed))

    def final(stage, landed, kind):
        take(zrecv.at[2 + kind], landed)
        total = stage[z].astype(f32)
        for d in range(7):
            total = total + landed[d].astype(f32)
        return total

    def cand_final(box, inbox, total, kind):
        take(crecv.at[4 + kind], inbox)
        total[...] = (
            box[zhi].astype(f32) + inbox[0].astype(f32) + inbox[1].astype(f32) + inbox[2].astype(f32)
        ).astype(bf16)

    FARTHEST = (3, 1, 2, 0)
    slot_terms(g_all, 1.0, dvc, cv_in, 0)
    for p in FARTHEST:
        terms(g_all, 1.0, dvb, dvown, rv, 0, p)

    for p in (1, 2, 3):
        take(mrecv.at[1, p], vq.at[p])
    for p in range(4):
        vpt[:, p * PART : (p + 1) * PART] = vq[p].reshape(PART, 128).astype(f32).T.astype(bf16)
    take(crecv.at[3], vc.at[0])
    slot_rows(vc, vs, vst)

    oc, dqc, pp = qc_in, gc_in, pp_in

    def attend(t, cand, i):
        at = columns(t, 256)
        out = nn(vpt[...], halves[:, at])
        if cand:
            out = out + nn(vst[i], slot_halves[:, at])
            out = jnp.where(cand_at[:, 0:256] < lengths[i], out, 0.0)
        delta = jnp.sum(out * g_all[at, :].astype(f32).T, axis=0, keepdims=True)
        deltas[:, at] = jnp.broadcast_to(delta, (8, 256))
        return out.T

    def put_cand(target, i, pair, rows):
        for a in range(2):
            for k in range(4):
                at = a * 128 + k * 32
                target[slots[i] * 4 + k, :, columns(pair * 2 + a, 128)] = rows[at : at + 32, :].astype(bf16)

    def give_back(kind, source, target, width, which):
        here = target.at[:, columns(g, width)]
        if 0 in which:
            start([pltpu.make_async_copy(source.at[j], here, brecv.at[kind])])
            late.append((bsend.at[kind], source.at[pl.ds(0, 7)]))
            late.append((brecv.at[kind], target))
        start([remote(source.at[flip(j, d)], here, bsend.at[kind], brecv.at[kind], block[d]) for d in which if d])

    OTHER, OWN = (4, 5, 6, 7), (1, 2, 3, 0)
    for i, which in enumerate((OTHER, OWN)):

        for pair in range(4):
            put_cand(oc, i, pair, attend(i * 4 + pair, True, i))
        give_back(0, oc, oc_out, 1024, which)

    for t in range(2):
        prompt_out[columns(t, 256), :] = attend(8 + t, False, None)

    def grade(values, turned, p, at):
        dw = nt(values, g_all[at, :])
        ds = (part_scores(p)[:, at] * shares[p, 0:1, at] * (dw - deltas[0:1, at])).astype(bf16)
        part_halves(p)[:, at] = ds
        return nn(turned, ds)

    for t in range(4):
        at = columns(t, WIDE)
        dq[:, at] = grade(vs[t // 2], kst[t // 2], 4, at)
    dq[:, 2048:] = jnp.zeros((128, WIDE), f32)
    slot_terms(q_all, SCALE, dkc, ck_in, 1)

    def grade_part(p, first, last):
        rows = slice(p * PART, (p + 1) * PART)

        for t in range(first, last):
            at = columns(t, WIDE)
            dq[:, at] += grade(vq[p].reshape(PART, 128), kpt[:, rows], p, at)

    for n, p in enumerate(FARTHEST[:3]):
        grade_part(p, 0, 5)
        terms(q_all, SCALE, dkb, dkown, rk, 1, p)
        if n == 0:
            along_z(dvown, rv, zv, zv_in, 0)
            cand_final(dvc, cv_in, cv_sum, 0)
            give_back(3, cv_sum, cv_out, 128, OTHER + OWN)
    vsum[...] = final(zv, zv_in, 0)
    for i, which in enumerate((OTHER, OWN)):
        grade_part(0, i * 2, i * 2 + 2)
        for pair in range(4):
            t = i * 4 + pair
            put_cand(dqc, i, pair, (dq[:, t * 256 : (t + 1) * 256] * SCALE).T)
        give_back(2, dqc, dqc_out, 1024, which)
    grade_part(0, 4, 5)
    terms(q_all, SCALE, dkb, dkown, rk, 1, 0)
    along_z(dkown, rk, zk, zk_in, 1)
    for t in range(2):
        out = prompt_out[t * 256 : (t + 1) * 256, :]
        grads = (dq[:, 2048 + t * 256 : 2304 + t * 256] * SCALE).T
        for h in range(4):
            rows = slice(h * 64, (h + 1) * 64)
            both = jnp.concatenate([out[rows].reshape(8, 8, 128), grads[rows].reshape(8, 8, 128)], axis=1)
            pp[:, :, (t * 4 + h) * 128 : (t * 4 + h + 1) * 128] = both.astype(bf16)
    give_back(1, pp, pp_out, 1024, OTHER + OWN)
    cand_final(dkc, ck_in, ck_sum, 1)
    give_back(4, ck_sum, ck_out, 128, OTHER + OWN)
    ksum = final(zk, zk_in, 1)
    both = jnp.concatenate([ksum.reshape(8, 8, 128), vsum[...].reshape(8, 8, 128)], axis=1)
    psum[...] = both.astype(bf16)
    give_back(5, psum, kvp_out, 128, OTHER + OWN)
    for sem, ref in late:
        take(sem, ref)


def finish_kernel(
    oc, dqc, pp, kvp, ck, cv, prompt_out, prompt_dq, prompt_dk, prompt_dv, oc_out, dqc_out, ck_out, cv_out,
    oc_in, dqc_in, pp_in, kvp_in, ck_in, cv_in, sems,
):
    arrive = [
        pltpu.make_async_copy(source, here, sems.at[i])
        for i, (source, here) in enumerate(
            ((oc, oc_in), (dqc, dqc_in), (pp, pp_in), (kvp, kvp_in), (ck, ck_in), (cv, cv_in))
        )
    ]
    start(arrive)
    leave = []
    for i, here, target in ((0, oc_in, oc_out), (1, dqc_in, dqc_out), (4, ck_in, ck_out), (5, cv_in, cv_out)):
        arrive[i].wait()
        leave.append(pltpu.make_async_copy(here, target, sems.at[6 + i]))
        leave[-1].start()
    for i, source, upper, lower in ((2, pp_in, prompt_out, prompt_dq), (3, kvp_in, prompt_dk, prompt_dv)):
        arrive[i].wait()
        both = source[...].astype(f32)
        upper[...] = both[0:8].astype(bf16)
        lower[...] = both[8:16].astype(bf16)
    for copy in leave:
        copy.wait()


ANY = pl.BlockSpec(memory_space=pl.ANY)
VMEM = pl.BlockSpec(memory_space=pltpu.VMEM)


def local(
    prompt_q, prompt_k, prompt_v, prompt_dout, cand_q, cand_k, cand_v, cand_dout, cand_len, placement
):
    DMA = pltpu.SemaphoreType.DMA

    def half(*shape):
        return pltpu.VMEM(shape, bf16)

    def full(*shape):
        return pltpu.VMEM(shape, f32)

    def result(*shape):
        return jax.ShapeDtypeStruct(shape, bf16)

    oc, dqc, pp, kvp, ck, cv = pl.pallas_call(
        kernel,
        out_shape=(
            result(32, 8192), result(32, 8192), result(16, 8192), result(16, 1024), result(32, 1024), result(32, 1024)
        ),
        in_specs=[ANY] * 2 + [VMEM] * 4 + [ANY] * 4,
        out_specs=(ANY,) * 6,
        scratch_shapes=[
            half(16, 8192), half(16, 1024), half(8, 16, 128), half(4, 8, 32, 128), half(4, 8, 32, 128),
            half(8, 32, 1024), half(8, 16, 1024), half(8, 32, 1024), half(4, 8, 64, 128), half(4, 8, 64, 128),
            half(LANES, 128), half(LANES, 128), half(2, SPAN, 128), half(2, SPAN, 128),
            half(128, PROMPT), half(128, PROMPT), half(2, 128, SPAN), half(2, 128, SPAN),
            full(PROMPT, LANES), half(PROMPT, LANES), full(SPAN, 2048), half(SPAN, 2048), full(5, 8, LANES), full(5, 8, LANES), full(8, LANES), full(512, 128), full(128, LANES),
            half(3, 8, 64, 128), half(3, 8, 64, 128), half(3, 8, 64, 128), half(3, 8, 64, 128),
            half(8, 64, 128), half(8, 64, 128), half(7, 64, 128), half(7, 64, 128),
            full(8, 64, 128), full(8, 64, 128), full(64, 128),
            half(4, 8, 32, 128), half(4, 8, 32, 128), half(3, 8, 32, 128), half(3, 8, 32, 128),
            half(8, 32, 128), half(8, 32, 128), half(8, 16, 128),
            pltpu.SMEM((16,), jnp.int32), pltpu.SMEM((16,), jnp.int32),
            DMA((2,)), DMA((6,)), DMA((6,)), DMA((4,)), DMA((6,)), DMA((4,)), DMA((4, 4)),
            DMA((6,)), DMA((6,)), DMA((6,)), DMA((6,)),
        ],
        compiler_params=pltpu.CompilerParams(
            collective_id=0, has_side_effects=True, vmem_limit_bytes=60 * 2**20
        ),
        name="layer",
    )(
        cand_len, placement,
        prompt_q, prompt_k, prompt_v, prompt_dout, cand_q, cand_k, cand_v, cand_dout,
    )
    return pl.pallas_call(
        finish_kernel,
        out_shape=(
            result(8, 8192), result(8, 8192), result(8, 1024), result(8, 1024),
            result(32, 8192), result(32, 8192), result(32, 1024), result(32, 1024),
        ),
        in_specs=[ANY] * 6,
        out_specs=(VMEM,) * 4 + (ANY,) * 4,
        scratch_shapes=[
            half(32, 8192), half(32, 8192), half(16, 8192), half(16, 1024), half(32, 1024), half(32, 1024), DMA((12,))
        ],
        name="finish",
    )(oc, dqc, pp, kvp, ck, cv)


def solution(mesh):
    rows = P(("seq", "head"), None)
    return jax.shard_map(
        local,
        mesh=mesh,
        in_specs=(rows,) * 8 + (P(), P()),
        out_specs=(rows,) * 8,
        check_vma=False,
    )
```

```python
import functools
import math

import jax
import jax.numpy as jnp
from jax import lax
from jax.experimental import pallas as pl
from jax.experimental.pallas import tpu as pltpu
from jax.sharding import PartitionSpec as P

HD = 128
SCALE = 1.0 / math.sqrt(HD)
SCALE2 = SCALE * math.log2(math.e)
MESH = pl.DeviceIdType.MESH
f32, bf16 = jnp.float32, jnp.bfloat16
HIDDEN = -1e30
PART = 512
PROMPT, SPAN = 2048, 512
KEYS = PROMPT + SPAN
LANES = 2560
WIDE = 512


def coords():
    seq, head = lax.axis_index("seq"), lax.axis_index("head")
    x, y = seq % 4, (seq // 4) % 4
    z = (head // 2) * 2 + seq // 16
    return x, y, z, head % 2


def device(x, y, z, core):
    return ((z % 2) * 16 + y * 4 + x, (z // 2) * 2 + core)


def roles(x, y, core):
    xg, sx, yg, sy = x // 2, x % 2, y // 2, y % 2
    j = sy * 4 + sx * 2 + core
    g = ((sy + yg) % 2) * 4 + ((sx + xg) % 2) * 2 + core
    return xg, yg, j, g


def flip(value, bits):
    out = 0
    for bit in (4, 2, 1):
        digit = (value // bit) % 2
        out = out + bit * ((1 - digit) if bits & bit else digit)
    return out


def block_partner(x, y, z, core, d):
    px = x // 2 * 2 + (1 - x % 2 if d & 2 else x % 2)
    py = y // 2 * 2 + (1 - y % 2 if d & 4 else y % 2)
    return device(px, py, z, 1 - core if d & 1 else core)


def greet(partners):
    barrier = pltpu.get_barrier_semaphore()
    for partner in partners:
        pl.semaphore_signal(barrier, inc=1, device_id=partner, device_id_type=MESH)
    pl.semaphore_wait(barrier, len(partners))


def remote(src, dst, send, recv, target):
    return pltpu.make_async_remote_copy(
        src_ref=src, dst_ref=dst, send_sem=send, recv_sem=recv, device_id=target, device_id_type=MESH
    )


def start(copies):
    for copy in copies:
        copy.start()


def take(sem, ref):
    pltpu.make_async_copy(ref, ref, sem).wait()


def nt(a, b):
    return lax.dot_general(a, b, (((1,), (1,)), ((), ())), preferred_element_type=f32)


def nn(a, b):
    return lax.dot_general(a, b, (((1,), (0,)), ((), ())), preferred_element_type=f32)


def columns(index, width):
    if isinstance(index, int):
        return pl.ds(index * width, width)
    return pl.ds(pl.multiple_of(index * width, width), width)


def kernel(
    cand_len_in, placement_in,
    prompt_q, prompt_k, prompt_v, prompt_dout, cand_q, cand_k, cand_v, cand_dout,
    oc_out, dqc_out, pp_out, kvp_out, ck_out, cv_out,
    pp_stage, kv_stage, kvp_in, kc, vc, qc_in, pp_in, gc_in, kq, vq,
    q_all, g_all, ks, vs, kpt, vpt, kst, vst,
    scores, halves, slot_scores, slot_halves, peaks, shares, deltas, prompt_out, dq,
    dvb, dkb, rv, rk, zv, zk, zv_in, zk_in, dvown, dkown, vsum,
    dvc, dkc, cv_in, ck_in, cv_sum, ck_sum, psum,
    cand_len, placement, lsem, asend, arecv, zsend, zrecv, msend, mrecv, csend, crecv, bsend, brecv,
):
    x, y, z, core = coords()
    xg, yg, j, g = roles(x, y, core)
    zhi, sy = z // 2, y % 2
    block = {d: block_partner(x, y, z, core, d) for d in range(1, 8)}
    mirror = {
        1: device(3 - x, y, z, core), 2: device(x, 3 - y, z, core), 3: device(3 - x, 3 - y, z, core)
    }
    column = {d: device(x, y, (z + d) % 8, core) for d in range(1, 8)}

    small = [
        pltpu.make_async_copy(cand_len_in, cand_len, lsem.at[0]),
        pltpu.make_async_copy(placement_in, placement, lsem.at[1]),
    ]
    start(small)
    both = jnp.concatenate([prompt_k[...].astype(f32), prompt_v[...].astype(f32)], axis=0)
    kv_stage[...] = both.astype(bf16)
    both = jnp.concatenate([prompt_q[...].astype(f32), prompt_dout[...].astype(f32)], axis=0)
    pp_stage[...] = both.astype(bf16)

    greet(list(block.values()) + list(mirror.values()) + list(column.values()))

    late = []

    def exchange(kind, source, width, target):
        start([pltpu.make_async_copy(source.at[:, columns(g, width)], target.at[j], arecv.at[kind])])
        start(
            [
                remote(source.at[:, columns(flip(g, d), width)], target.at[j], asend.at[kind], arecv.at[kind], block[d])
                for d in range(1, 8)
            ]
        )
        late.append((asend.at[kind], target.at[pl.ds(0, 7)]))

    exchange(0, kv_stage, 128, kvp_in)
    exchange(1, cand_k, 128, kc.at[zhi])
    exchange(2, cand_q, 1024, qc_in)
    exchange(3, pp_stage, 1024, pp_in)
    exchange(4, cand_v, 128, vc.at[zhi])
    exchange(5, cand_dout, 1024, gc_in)

    CLOSE, DISTANT = (1, 7, 2, 6), (3, 5, 4)
    below, above = (zhi + 3) % 4, (zhi + 1) % 4
    first, second = pl.ds(0, 4), pl.ds(4, 4)

    def along_z_in(which, kind):
        start(
            [
                remote(
                    which.at[0, z], which.at[0, z], zsend.at[kind],
                    zrecv.at[kind if d in CLOSE else 4 + kind], column[d],
                )
                for d in CLOSE + DISTANT
            ]
        )
        late.append((zsend.at[kind], which.at[0, pl.ds(0, 7)]))

    def forward(which, kind, steps):
        for d in steps:
            at = (z + 8 - d) % 8
            start([remote(which.at[0, at], which.at[p, at], msend.at[kind], mrecv.at[kind, p], mirror[p]) for p in (1, 2, 3)])

    def quadrants(which, kind):
        forward(which, kind, (0,))
        take(zrecv.at[kind], which.at[0, pl.ds(0, 4)])
        forward(which, kind, CLOSE)
        take(zrecv.at[4 + kind], which.at[0, pl.ds(0, 3)])
        forward(which, kind, DISTANT)
        late.append((msend.at[kind], which.at[pl.ds(0, 3)]))

    def near(which, kind):
        take(arecv.at[1 + 3 * kind], which.at[zhi])
        start(
            [
                remote(which.at[zhi], which.at[zhi], csend.at[kind], crecv.at[kind], column[d])
                for d in (2, 6)
            ]
        )
        late.append((csend.at[kind], which.at[pl.ds(0, 2)]))

    def far(which, kind):
        take(crecv.at[kind], which.at[pl.ds(0, 2)])
        start(
            [
                remote(which.at[below, first], which.at[below, first], csend.at[2 + kind], crecv.at[2 + kind], column[2]),
                remote(which.at[above, second], which.at[above, second], csend.at[2 + kind], crecv.at[2 + kind], column[6]),
            ]
        )
        late.append((csend.at[2 + kind], which.at[0]))

    take(arecv.at[0], kvp_in)
    both = kvp_in[...].astype(f32)
    kq[0, z] = both[:, 0:8, :].reshape(64, 128).astype(bf16)
    vq[0, z] = both[:, 8:16, :].reshape(64, 128).astype(bf16)
    along_z_in(kq, 0)
    along_z_in(vq, 1)
    near(kc, 0)
    quadrants(kq, 0)
    quadrants(vq, 1)
    far(kc, 0)
    near(vc, 1)

    slots = (1 - sy, sy)
    take(arecv.at[2], qc_in)
    for i in range(2):
        for k in range(4):
            rows = qc_in[slots[i] * 4 + k]
            for h in range(8):
                at = i * 1024 + h * 128 + k * 32
                q_all[at : at + 32, :] = rows[:, h * 128 : (h + 1) * 128]
    take(arecv.at[3], pp_in)
    for h in range(8):
        both = pp_in[:, :, h * 128 : (h + 1) * 128].astype(f32)
        at = 2048 + h * 64
        q_all[at : at + 64, :] = both[:, 0:8, :].reshape(64, 128).astype(bf16)
        g_all[at : at + 64, :] = both[:, 8:16, :].reshape(64, 128).astype(bf16)

    lane = lax.broadcasted_iota(jnp.int32, (1, WIDE), 1)
    cand_at = ((lane // 64) % 2) * 256 + zhi * 64 + lane % 64
    prompt_at = (
        (z % 2) * 1024 + zhi * 16 + yg * 512 + xg * 128
        + ((lane // 32) % 2) * 256 + ((lane // 16) % 2) * 64 + ((lane // 8) % 2) * 8 + lane % 8
    )

    def part_scores(p):
        return slot_scores if p == 4 else scores.at[p * PART : (p + 1) * PART]

    def part_halves(p):
        return slot_halves if p == 4 else halves.at[p * PART : (p + 1) * PART]

    def weigh_part(p, at, s):
        peak = jnp.max(jnp.max(s.reshape(-1, 8, WIDE), axis=0), axis=0, keepdims=True)
        e = jnp.exp2((s - peak) * SCALE2)
        part_scores(p)[:, at] = e
        peaks[p, :, at] = jnp.broadcast_to(peak, (8, WIDE))
        shares[p, :, at] = jnp.sum(e.reshape(-1, 8, WIDE), axis=0)

    def score_part(p):
        rows = slice(p * PART, (p + 1) * PART)
        keys = kq[p].reshape(PART, 128)

        def cand(t, carry):
            at = columns(t, WIDE)
            weigh_part(p, at, nt(keys, q_all[at, :]))
            return carry

        lax.fori_loop(0, 4, cand, 0, unroll=4)
        n = lax.broadcasted_iota(jnp.int32, (PART, 1), 0)
        zz = n // 64
        ygp = yg if p < 2 else 1 - yg
        xgp = xg if p % 2 == 0 else 1 - xg
        key_at = (
            (zz % 2) * 1024 + (zz // 2) * 16 + ygp * 512 + ((n // 32) % 2) * 256
            + xgp * 128 + ((n // 16) % 2) * 64 + ((n // 8) % 2) * 8 + n % 8
        )

        weigh_part(p, pl.ds(2048, WIDE), jnp.where(key_at <= prompt_at, nt(keys, q_all[2048:, :]), HIDDEN))
        kpt[:, rows] = keys.astype(f32).T.astype(bf16)

    score_part(0)
    for p in (1, 2, 3):
        take(mrecv.at[0, p], kq.at[p])
        score_part(p)

    def slot_rows(source, target, turned):
        for i in range(2):
            for half in range(2):
                for hi in range(4):
                    for c in range(2):
                        at = half * 256 + hi * 64 + c * 32
                        target[i, at : at + 32, :] = source[hi, slots[i] * 4 + half * 2 + c]
            turned[i] = target[i].astype(f32).T.astype(bf16)

    far(vc, 1)
    take(crecv.at[2], kc.at[0])
    slot_rows(kc, ks, kst)
    span_at = lax.broadcasted_iota(jnp.int32, (SPAN, 1), 0)

    def score_slot(t, carry):
        at = columns(t, WIDE)
        weigh_part(4, at, jnp.where(span_at <= cand_at, nt(ks[t // 2], q_all[at, :]), HIDDEN))
        return carry

    lax.fori_loop(0, 4, score_slot, 0, unroll=2)

    def weigh(t, parts):
        at = columns(t, WIDE)
        tops = [peaks[p, 0:1, at] for p in range(parts)]
        peak = functools.reduce(jnp.maximum, tops)
        lifts = [jnp.exp2((top - peak) * SCALE2) for top in tops]
        sums = [jnp.sum(shares[p, :, at], axis=0, keepdims=True) for p in range(parts)]
        share = 1.0 / sum(lift * total for lift, total in zip(lifts, sums))
        for p in range(parts):
            lift = lifts[p] * share
            shares[p, :, at] = jnp.broadcast_to(lift, (8, WIDE))
            part_halves(p)[:, at] = (part_scores(p)[:, at] * lift).astype(bf16)

    for t in range(4):
        weigh(t, KEYS // PART)
    weigh(4, PROMPT // PART)

    small[0].wait()
    small[1].wait()
    lengths = []
    for i in range(2):
        slot = (z % 2) * 8 + ((y // 2) * 2 + slots[i]) * 2 + x // 2
        length = jnp.int32(0)
        for c in range(16):
            length = length + jnp.where(placement[c] == slot, cand_len[c], 0)
        lengths.append(length)
    take(arecv.at[5], gc_in)
    row = lax.broadcasted_iota(jnp.int32, (32, 1), 0)
    for i in range(2):
        for k in range(4):
            kept = (k // 2) * 256 + zhi * 64 + (k % 2) * 32 + row < lengths[i]
            rows = jnp.where(kept, gc_in[slots[i] * 4 + k].astype(f32), 0.0).astype(bf16)
            for h in range(8):
                at = i * 1024 + h * 128 + k * 32
                g_all[at : at + 32, :] = rows[:, h * 128 : (h + 1) * 128]
    def cand_terms(sums, target, i):
        for half in range(2):
            for hi in range(4):
                for c in range(2):
                    at = half * 256 + hi * 64 + c * 32
                    target[hi, slots[i] * 4 + half * 2 + c] = sums[at : at + 32, :].astype(bf16)

    def slot_terms(others, scale, box, inbox, kind):
        for i in range(2):
            rows = slice(i * 1024, (i + 1) * 1024)
            cand_terms(nn(slot_halves[:, rows], others[rows, :]) * scale, box, i)
        start(
            [
                remote(box.at[(zhi + n) % 4], inbox.at[n - 1], csend.at[4 + kind], crecv.at[4 + kind], column[2 * n])
                for n in (1, 2, 3)
            ]
        )
        late.append((csend.at[4 + kind], inbox))

    def terms(others, scale, boxes, mine, inbox, kind, p):
        total = nn(halves[p * PART : (p + 1) * PART, :], others[...]) * scale
        if p == 0:
            mine[...] = total.reshape(8, 64, 128)
            late.append((msend.at[2 + kind], inbox))
            return
        boxes[p - 1] = total.reshape(8, 64, 128).astype(bf16)
        start([remote(boxes.at[p - 1], inbox.at[p - 1], msend.at[2 + kind], mrecv.at[2 + kind, 0], mirror[p])])

    def along_z(mine, inbox, stage, landed, kind):
        take(mrecv.at[2 + kind, 0], inbox)
        total = mine[...] + inbox[0].astype(f32) + inbox[1].astype(f32) + inbox[2].astype(f32)
        stage[...] = total.astype(bf16)
        start(
            [
                remote(stage.at[(z + d) % 8], landed.at[d - 1], zsend.at[2 + kind], zrecv.at[2 + kind], column[d])
                for d in (4, 3, 5, 2, 6, 1, 7)
            ]
        )
        late.append((zsend.at[2 + kind], landed))

    def final(stage, landed, kind):
        take(zrecv.at[2 + kind], landed)
        total = stage[z].astype(f32)
        for d in range(7):
            total = total + landed[d].astype(f32)
        return total

    def cand_final(box, inbox, total, kind):
        take(crecv.at[4 + kind], inbox)
        total[...] = (
            box[zhi].astype(f32) + inbox[0].astype(f32) + inbox[1].astype(f32) + inbox[2].astype(f32)
        ).astype(bf16)

    FARTHEST = (3, 1, 2, 0)
    slot_terms(g_all, 1.0, dvc, cv_in, 0)
    for p in FARTHEST:
        terms(g_all, 1.0, dvb, dvown, rv, 0, p)

    for p in (1, 2, 3):
        take(mrecv.at[1, p], vq.at[p])
    for p in range(4):
        vpt[:, p * PART : (p + 1) * PART] = vq[p].reshape(PART, 128).astype(f32).T.astype(bf16)
    take(crecv.at[3], vc.at[0])
    slot_rows(vc, vs, vst)

    oc, dqc, pp = qc_in, gc_in, pp_in

    def attend(t, cand, i):
        at = columns(t, 256)
        out = nn(vpt[...], halves[:, at])
        if cand:
            out = out + nn(vst[i], slot_halves[:, at])
            out = jnp.where(cand_at[:, 0:256] < lengths[i], out, 0.0)
        delta = jnp.sum(out * g_all[at, :].astype(f32).T, axis=0, keepdims=True)
        deltas[:, at] = jnp.broadcast_to(delta, (8, 256))
        return out.T

    def put_cand(target, i, pair, rows):
        for a in range(2):
            for k in range(4):
                at = a * 128 + k * 32
                target[slots[i] * 4 + k, :, columns(pair * 2 + a, 128)] = rows[at : at + 32, :].astype(bf16)

    def give_back(kind, source, target, width, which):
        here = target.at[:, columns(g, width)]
        if 0 in which:
            start([pltpu.make_async_copy(source.at[j], here, brecv.at[kind])])
            late.append((bsend.at[kind], source.at[pl.ds(0, 7)]))
            late.append((brecv.at[kind], target))
        start([remote(source.at[flip(j, d)], here, bsend.at[kind], brecv.at[kind], block[d]) for d in which if d])

    OTHER, OWN = (4, 5, 6, 7), (1, 2, 3, 0)
    for i, which in enumerate((OTHER, OWN)):

        for pair in range(4):
            put_cand(oc, i, pair, attend(i * 4 + pair, True, i))
        give_back(0, oc, oc_out, 1024, which)

    for t in range(2):
        prompt_out[columns(t, 256), :] = attend(8 + t, False, None)

    def grade(values, turned, p, at):
        dw = nt(values, g_all[at, :])
        ds = (part_scores(p)[:, at] * shares[p, 0:1, at] * (dw - deltas[0:1, at])).astype(bf16)
        part_halves(p)[:, at] = ds
        return nn(turned, ds)

    for t in range(4):
        at = columns(t, WIDE)
        dq[:, at] = grade(vs[t // 2], kst[t // 2], 4, at)
    dq[:, 2048:] = jnp.zeros((128, WIDE), f32)
    slot_terms(q_all, SCALE, dkc, ck_in, 1)

    def grade_part(p, first, last):
        rows = slice(p * PART, (p + 1) * PART)

        for t in range(first, last):
            at = columns(t, WIDE)
            dq[:, at] += grade(vq[p].reshape(PART, 128), kpt[:, rows], p, at)

    for n, p in enumerate(FARTHEST[:3]):
        grade_part(p, 0, 5)
        terms(q_all, SCALE, dkb, dkown, rk, 1, p)
        if n == 0:
            along_z(dvown, rv, zv, zv_in, 0)
            cand_final(dvc, cv_in, cv_sum, 0)
            give_back(3, cv_sum, cv_out, 128, OTHER + OWN)
    vsum[...] = final(zv, zv_in, 0)
    for i, which in enumerate((OTHER, OWN)):
        grade_part(0, i * 2, i * 2 + 2)
        for pair in range(4):
            t = i * 4 + pair
            put_cand(dqc, i, pair, (dq[:, t * 256 : (t + 1) * 256] * SCALE).T)
        give_back(2, dqc, dqc_out, 1024, which)
    grade_part(0, 4, 5)
    terms(q_all, SCALE, dkb, dkown, rk, 1, 0)
    along_z(dkown, rk, zk, zk_in, 1)
    for t in range(2):
        out = prompt_out[t * 256 : (t + 1) * 256, :]
        grads = (dq[:, 2048 + t * 256 : 2304 + t * 256] * SCALE).T
        for h in range(4):
            rows = slice(h * 64, (h + 1) * 64)
            both = jnp.concatenate([out[rows].reshape(8, 8, 128), grads[rows].reshape(8, 8, 128)], axis=1)
            pp[:, :, (t * 4 + h) * 128 : (t * 4 + h + 1) * 128] = both.astype(bf16)
    give_back(1, pp, pp_out, 1024, OTHER + OWN)
    cand_final(dkc, ck_in, ck_sum, 1)
    give_back(4, ck_sum, ck_out, 128, OTHER + OWN)
    ksum = final(zk, zk_in, 1)
    both = jnp.concatenate([ksum.reshape(8, 8, 128), vsum[...].reshape(8, 8, 128)], axis=1)
    psum[...] = both.astype(bf16)
    give_back(5, psum, kvp_out, 128, OTHER + OWN)
    for sem, ref in late:
        take(sem, ref)


def finish_kernel(
    oc, dqc, pp, kvp, ck, cv, prompt_out, prompt_dq, prompt_dk, prompt_dv, oc_out, dqc_out, ck_out, cv_out,
    oc_in, dqc_in, pp_in, kvp_in, ck_in, cv_in, sems,
):
    arrive = [
        pltpu.make_async_copy(source, here, sems.at[i])
        for i, (source, here) in enumerate(
            ((oc, oc_in), (dqc, dqc_in), (pp, pp_in), (kvp, kvp_in), (ck, ck_in), (cv, cv_in))
        )
    ]
    start(arrive)
    leave = []
    for i, here, target in ((0, oc_in, oc_out), (1, dqc_in, dqc_out), (4, ck_in, ck_out), (5, cv_in, cv_out)):
        arrive[i].wait()
        leave.append(pltpu.make_async_copy(here, target, sems.at[6 + i]))
        leave[-1].start()
    for i, source, upper, lower in ((2, pp_in, prompt_out, prompt_dq), (3, kvp_in, prompt_dk, prompt_dv)):
        arrive[i].wait()
        both = source[...].astype(f32)
        upper[...] = both[0:8].astype(bf16)
        lower[...] = both[8:16].astype(bf16)
    for copy in leave:
        copy.wait()


ANY = pl.BlockSpec(memory_space=pl.ANY)
VMEM = pl.BlockSpec(memory_space=pltpu.VMEM)


def local(
    prompt_q, prompt_k, prompt_v, prompt_dout, cand_q, cand_k, cand_v, cand_dout, cand_len, placement
):
    DMA = pltpu.SemaphoreType.DMA

    def half(*shape):
        return pltpu.VMEM(shape, bf16)

    def full(*shape):
        return pltpu.VMEM(shape, f32)

    def result(*shape):
        return jax.ShapeDtypeStruct(shape, bf16)

    oc, dqc, pp, kvp, ck, cv = pl.pallas_call(
        kernel,
        out_shape=(
            result(32, 8192), result(32, 8192), result(16, 8192), result(16, 1024), result(32, 1024), result(32, 1024)
        ),
        in_specs=[ANY] * 2 + [VMEM] * 4 + [ANY] * 4,
        out_specs=(ANY,) * 6,
        scratch_shapes=[
            half(16, 8192), half(16, 1024), half(8, 16, 128), half(4, 8, 32, 128), half(4, 8, 32, 128),
            half(8, 32, 1024), half(8, 16, 1024), half(8, 32, 1024), half(4, 8, 64, 128), half(4, 8, 64, 128),
            half(LANES, 128), half(LANES, 128), half(2, SPAN, 128), half(2, SPAN, 128),
            half(128, PROMPT), half(128, PROMPT), half(2, 128, SPAN), half(2, 128, SPAN),
            full(PROMPT, LANES), half(PROMPT, LANES), full(SPAN, 2048), half(SPAN, 2048), full(5, 8, LANES), full(5, 8, LANES), full(8, LANES), full(512, 128), full(128, LANES),
            half(3, 8, 64, 128), half(3, 8, 64, 128), half(3, 8, 64, 128), half(3, 8, 64, 128),
            half(8, 64, 128), half(8, 64, 128), half(7, 64, 128), half(7, 64, 128),
            full(8, 64, 128), full(8, 64, 128), full(64, 128),
            half(4, 8, 32, 128), half(4, 8, 32, 128), half(3, 8, 32, 128), half(3, 8, 32, 128),
            half(8, 32, 128), half(8, 32, 128), half(8, 16, 128),
            pltpu.SMEM((16,), jnp.int32), pltpu.SMEM((16,), jnp.int32),
            DMA((2,)), DMA((6,)), DMA((6,)), DMA((4,)), DMA((6,)), DMA((4,)), DMA((4, 4)),
            DMA((6,)), DMA((6,)), DMA((6,)), DMA((6,)),
        ],
        compiler_params=pltpu.CompilerParams(
            collective_id=0, has_side_effects=True, vmem_limit_bytes=60 * 2**20
        ),
        name="layer",
    )(
        cand_len, placement,
        prompt_q, prompt_k, prompt_v, prompt_dout, cand_q, cand_k, cand_v, cand_dout,
    )
    return pl.pallas_call(
        finish_kernel,
        out_shape=(
            result(8, 8192), result(8, 8192), result(8, 1024), result(8, 1024),
            result(32, 8192), result(32, 8192), result(32, 1024), result(32, 1024),
        ),
        in_specs=[ANY] * 6,
        out_specs=(VMEM,) * 4 + (ANY,) * 4,
        scratch_shapes=[
            half(32, 8192), half(32, 8192), half(16, 8192), half(16, 1024), half(32, 1024), half(32, 1024), DMA((12,))
        ],
        name="finish",
    )(oc, dqc, pp, kvp, ck, cv)


def solution(mesh):
    rows = P(("seq", "head"), None)
    return jax.shard_map(
        local,
        mesh=mesh,
        in_specs=(rows,) * 8 + (P(), P()),
        out_specs=(rows,) * 8,
        check_vma=False,
    )
```
